128 devices in a mesh: pool: 2 (over core), dev: 64 (over x, z, y).
Axes of the slice: x: 4, y: 4, z: 4, core: 2. Of those that a mesh axis runs over, the one named last changes fastest.
Arguments:
- hidden: bfloat16 [2048, 4096], P(('pool', 'dev')), may hold values from -6 to 6
- queries: bfloat16 [2048, 8192], P(('pool', 'dev')), may hold values from -160 to 160
- k_cache: bfloat16 [2048, 128, 512], P(('pool', 'dev')), may hold values from -6 to 6
- v_cache: bfloat16 [2048, 128, 512], P(('pool', 'dev')), may hold values from -6 to 6
- o_weight: bfloat16 [8192, 4096], P('dev'), may hold values from -0.125 to 0.125
- norm_gain: bfloat16 [4096], replicated, may hold values from 0.25 to 1.75
- router_weight: bfloat16 [4096, 128], replicated, may hold values from -0.1875 to 0.1875
- w_gate: bfloat16 [128, 4096, 768], P(('pool', 'dev')), may hold values from -0.09375 to 0.09375
- w_up: bfloat16 [128, 4096, 768], P(('pool', 'dev')), may hold values from -0.09375 to 0.09375
- w_down: bfloat16 [128, 768, 4096], P(('pool', 'dev')), may hold values from -0.4375 to 0.4375
- routes: int32 [2048, 8], P(('pool', 'dev')), may hold values from 0 to 127, all different within a row; in each aligned block of 16 rows (0 to 15, 16 to 31, ...) at most 2 rows name the same one
Outputs:
- layer_out: bfloat16 [2048, 4096], P(('pool', 'dev'))
The draws below stay inside these ranges and needn't reach their ends.
Inputs may be any that keep to these rules, and one draw needn't show every extreme that they name: `routes`: each token names 8 different experts; among the 16 tokens of one device no expert is named more than 2 times.
All inputs are finite; a program needn't handle non-finite values.
Results may differ from the reference program's by a relative error of at most 0.023.
Values may be sent and summed in bfloat16 or wider, within the bound.
A program may use at most 128 MiB of HBM per device.

```python
import math
import jax
import jax.numpy as jnp
import numpy as np
from jax import lax

D = 4096
QH = 64
KVH = 4
HD = 128
TOPK = 8
HID = 768
TOK_DEV = 16
CTX = 128
EXPERTS = 128
TOKENS = 2048
MOST = 2
N_POOL = 2
N_DEV = 64


def base_keys(key):
    return jnp.clip(jax.random.normal(key, (TOKENS, CTX, KVH * HD), jnp.float32), -6.0, 6.0)


def draw_k_cache(key, part):
    keys_base = base_keys(key)
    return keys_base.astype(jnp.bfloat16)


def draw_queries(key, part):
    key = jax.random.fold_in(key, 7)
    per_group = QH // KVH
    values_out = jnp.clip(jax.random.normal(key, (TOKENS, KVH, per_group, HD), jnp.float32), -6.0, 6.0)
    return values_out.reshape(TOKENS, QH * HD).astype(jnp.bfloat16)


def steps_of(key, extent, cuts, least, top_value):
    def one(dim, parts):
        steps = jax.random.uniform(jax.random.fold_in(jax.random.fold_in(key, 6), dim), (parts,), jnp.float32, least / len(cuts), top_value / len(cuts))
        return jnp.repeat(jnp.exp(steps), extent[dim] // parts).reshape((-1,) + (1,) * (len(extent) - dim - 1))

    loudness = one(*cuts[0])
    for cut in cuts[1:]:
        loudness = loudness * one(*cut)
    return loudness


def shared_out(rng, own, number, rows, amount, top, reach, slope):
    sequence = jax.random.permutation(rng, amount)
    heavy_load, usual = shares(amount, rows * top, reach, slope, True), shares(amount, rows * top, reach, slope, False)
    places = jnp.arange(amount)

    def named(tallies, rotation):
        used = int((tallies > 0).sum())
        fixed = max(1, used // 4)
        shifted = fixed + (places - fixed + rotation * (used - fixed)) % max(1, amount - fixed)
        return jnp.zeros((amount,), jnp.int32).at[sequence[jnp.where(places < fixed, places, shifted)]].set(jnp.asarray(tallies, jnp.int32))

    tallies = jnp.where(number % 4 == 0, named(heavy_load, number // 4), named(usual, number - number // 4 - 1))
    mixed = jax.random.permutation(jax.random.fold_in(own, 3), amount)
    donor, taker = mixed[0:amount // 2 * 2:2], mixed[1:amount // 2 * 2:2]
    room = jnp.minimum(tallies[donor] - 1, reach - tallies[taker]) // 2
    room = jnp.where((donor == sequence[0]) | (taker == sequence[0]) | (tallies[taker] == 0), 0, jnp.maximum(room, 0))
    shifted = jax.random.randint(jax.random.fold_in(own, 4), (amount // 2,), 0, 1 << 20) % (room + 1)
    tallies = tallies.at[donor].add(-shifted).at[taker].add(shifted)
    members = jnp.searchsorted(jnp.cumsum(tallies), jnp.arange(rows * top), side="right").astype(jnp.int32)
    grid = members.reshape(top, rows).T
    grid = grid[jax.random.permutation(jax.random.fold_in(own, 1), rows)]
    rotation = jax.random.randint(jax.random.fold_in(own, 2), (rows, 1), 0, top)
    return jnp.take_along_axis(grid, (jnp.arange(top)[None, :] + rotation) % top, axis=1)


def shares(amount, total, most, skew, full):
    loads = [(1 << 20) // math.isqrt(rank ** skew) + 1 for rank in range(1, amount + 1)]
    largest = most if full else min(most, max(-(-total // amount), total * loads[0] // sum(loads)))
    least = 1 if total - largest >= amount - 1 else 0
    given, rest = [largest] + [least] * (amount - 1), total - largest - least * (amount - 1)
    while rest > 0:
        movable = [i for i in range(1, amount) if given[i] < largest] or [i for i in range(1, amount) if given[i] < most]
        mass, budget = sum([loads[i] for i in movable]), rest
        for i in movable:
            extra = min(most - given[i], max(1, budget * loads[i] // mass), rest)
            given[i] = given[i] + extra
            rest = rest - extra
    return np.array(given)


def bell_draw(rng, extent, deviation, bound, pieces=(), held_as=jnp.bfloat16):
    result = jax.random.normal(rng, extent, jnp.float32) * deviation
    if len(pieces) > 0:
        result = steps_of(rng, extent, pieces, -0.22, 0.18) * result
    return jnp.clip(result, min=-bound, max=bound).astype(held_as)


def setup_inputs(seed: int = 0) -> dict:
    key_of = jax.random.split(jax.random.key(seed), 12)
    hidden = bell_draw(key_of[0], (TOKENS, D), 1.0, 6.0, ((0, 128),))
    queries = draw_queries(jax.random.fold_in(key_of[11], 71), 0)
    k_cache = draw_k_cache(jax.random.fold_in(key_of[11], 71), 0)
    v_cache = bell_draw(key_of[3], (TOKENS, CTX, KVH * HD), 1.0, 6.0, ((0, 128),))
    o_weight = bell_draw(key_of[4], (QH * HD, D), (QH * HD // 4) ** -0.5, 0.125, ((0, 64),))
    norm_gain = jnp.clip(1.0 + 0.15 * jax.random.normal(key_of[5], (D,), jnp.float32), 0.25, 1.75).astype(jnp.bfloat16)
    router_weight = bell_draw(key_of[6], (D, EXPERTS), (D // 4) ** -0.5, 0.1875)
    w_gate = bell_draw(key_of[7], (EXPERTS, D, HID), D ** -0.5, 0.09375, ((0, 128),))
    w_up = bell_draw(key_of[8], (EXPERTS, D, HID), D ** -0.5, 0.09375, ((0, 128),))
    w_down = bell_draw(key_of[9], (EXPERTS, HID, D), (HID // 4) ** -0.5, 0.4375, ((0, 128),))
    routes_keys = jax.random.split(jax.random.fold_in(key_of[10], 1), TOKENS // TOK_DEV)
    routes_turns = jax.random.permutation(jax.random.fold_in(key_of[10], 3), TOKENS // TOK_DEV)
    routes = jax.vmap(lambda own, number: shared_out(jax.random.fold_in(key_of[10], 2), own, number, TOK_DEV, EXPERTS, TOPK, MOST, 2))(routes_keys, routes_turns).reshape((TOKENS, TOPK))
    return dict(hidden=hidden, queries=queries, k_cache=k_cache, v_cache=v_cache, o_weight=o_weight, norm_gain=norm_gain, router_weight=router_weight, w_gate=w_gate, w_up=w_up, w_down=w_down, routes=routes)


def expert_rows(inputs, gate_weight, up_weight, down_weight):
    gate_value = jnp.dot(inputs, gate_weight, preferred_element_type=jnp.float32)
    up_value = jnp.dot(inputs, up_weight, preferred_element_type=jnp.float32)
    activated = (jax.nn.silu(gate_value) * up_value).astype(jnp.bfloat16)
    return jnp.dot(activated, down_weight, preferred_element_type=jnp.float32).astype(jnp.bfloat16)

def reference(hidden, queries, k_cache, v_cache, o_weight, norm_gain, router_weight, w_gate, w_up, w_down, routes):
    per_group = QH // KVH
    query_f = queries.astype(jnp.float32).reshape(TOKENS, KVH, per_group, HD)
    key_f = k_cache.astype(jnp.float32).reshape(TOKENS, CTX, KVH, HD)
    value_f = v_cache.astype(jnp.float32).reshape(TOKENS, CTX, KVH, HD)
    scores = jnp.einsum('tgqd,tcgd->tgqc', query_f, key_f) / math.sqrt(HD)
    attn_probs = jax.nn.softmax(scores, axis=-1).astype(jnp.bfloat16)
    attended = jnp.einsum('tgqc,tcgd->tgqd', attn_probs.astype(jnp.float32), value_f)
    attended = attended.astype(jnp.bfloat16).reshape(TOKENS, QH * HD)
    project = jnp.dot(attended, o_weight, preferred_element_type=jnp.float32)
    residual = (hidden.astype(jnp.float32) + project).astype(jnp.bfloat16)
    resid_f = residual.astype(jnp.float32)
    mean_square = lax.optimization_barrier(jnp.mean(resid_f * resid_f, axis=-1, keepdims=True))
    normed = (resid_f * lax.rsqrt(mean_square + 1e-06) * norm_gain.astype(jnp.float32)).astype(jnp.bfloat16)
    logits = jnp.dot(normed, router_weight, preferred_element_type=jnp.float32)
    chosen = jnp.take_along_axis(logits, routes, axis=1)
    weights = jax.nn.softmax(chosen, axis=-1)
    capacity = N_POOL * N_DEV * MOST

    def visit(running, expert):
        member = routes == expert
        route_share = lax.optimization_barrier(jnp.sum(jnp.where(member, weights, jnp.zeros_like(weights)), axis=1))
        picked = jnp.any(member, axis=1)
        rows_at = jnp.nonzero(picked, size=capacity, fill_value=0)[0].astype(jnp.int32)
        outputs = expert_rows(normed[rows_at], w_gate[expert], w_up[expert], w_down[expert])
        live = jnp.arange(capacity) < jnp.sum(picked.astype(jnp.int32))
        scaled_share = jnp.where(live, route_share[rows_at], jnp.zeros_like(route_share[rows_at]))
        return (running.at[rows_at].add(scaled_share[:, None] * outputs.astype(jnp.float32)), None)
    mixture, _ = lax.scan(visit, jnp.zeros((TOKENS, D), jnp.float32), jnp.arange(EXPERTS).astype(jnp.int32))
    return (resid_f + mixture).astype(jnp.bfloat16)
```

```python
import math

import jax
import jax.numpy as jnp
from jax import lax
from jax.sharding import PartitionSpec as P

QH = 64
KVH = 4
HD = 128
TOPK = 8
LINE = 4
PLANE = 16
LINES = [[LINE * i + j for j in range(LINE)] for i in range(PLANE)]
PLANES = [[LINE * i + j for i in range(PLANE)] for j in range(LINE)]


def expert_rows(inputs, gate_weight, up_weight, down_weight):
    gate_value = jnp.dot(inputs, gate_weight, preferred_element_type=jnp.float32)
    up_value = jnp.dot(inputs, up_weight, preferred_element_type=jnp.float32)
    activated = (jax.nn.silu(gate_value) * up_value).astype(jnp.bfloat16)
    return jnp.dot(activated, down_weight, preferred_element_type=jnp.float32).astype(jnp.bfloat16)


def expert_block(received, gate_weight, up_weight, down_weight):
    flat_rows = received.reshape(-1, received.shape[-1])
    return expert_rows(flat_rows, gate_weight, up_weight, down_weight).reshape(received.shape)


def shards(
    hidden,
    queries,
    k_cache,
    v_cache,
    o_weight,
    norm_gain,
    router_weight,
    w_gate,
    w_up,
    w_down,
    routes,
):
    tok_rows = hidden.shape[0]
    model_width = hidden.shape[1]
    per_group = QH // KVH
    query_b = queries.reshape(tok_rows, KVH, per_group, HD)
    key_b = k_cache.reshape(tok_rows, -1, KVH, HD)
    value_b = v_cache.reshape(tok_rows, -1, KVH, HD)
    scores = jnp.einsum(
        "tgqd,tcgd->tgqc", query_b, key_b, preferred_element_type=jnp.float32
    ) / math.sqrt(HD)
    attn_probs = jax.nn.softmax(scores, axis=-1).astype(jnp.bfloat16)
    attended = jnp.einsum(
        "tgqc,tcgd->tgqd", attn_probs, value_b, preferred_element_type=jnp.float32
    )
    attended = attended.astype(jnp.bfloat16).reshape(tok_rows, PLANE, -1)
    by_head = lax.all_to_all(
        attended, "dev", split_axis=1, concat_axis=0, tiled=True, axis_index_groups=PLANES
    )
    head_rows = by_head.reshape(PLANE * tok_rows, -1)
    wide = lax.all_gather(o_weight, "dev", axis_index_groups=LINES, tiled=True)
    partial = jnp.dot(head_rows, wide, preferred_element_type=jnp.float32).astype(jnp.bfloat16)
    shares = lax.all_to_all(
        partial.reshape(PLANE, tok_rows, -1),
        "dev",
        split_axis=0,
        concat_axis=0,
        tiled=True,
        axis_index_groups=PLANES,
    )
    project = jnp.sum(shares.astype(jnp.float32), axis=0)
    residual = (hidden.astype(jnp.float32) + project).astype(jnp.bfloat16)
    resid_f = residual.astype(jnp.float32)
    mean_square = jnp.mean(resid_f * resid_f, axis=-1, keepdims=True)
    normed = (resid_f * lax.rsqrt(mean_square + 1e-06) * norm_gain.astype(jnp.float32)).astype(
        jnp.bfloat16
    )
    logits = jnp.dot(normed, router_weight, preferred_element_type=jnp.float32)
    chosen = jnp.take_along_axis(logits, routes, axis=1)
    weights = jax.nn.softmax(chosen, axis=-1)
    experts_all = router_weight.shape[1]
    slot_count = max(2, 2 * tok_rows * TOPK // experts_all)
    flat_ids = routes.reshape(-1)
    onehot = (flat_ids[:, None] == jnp.arange(experts_all)[None, :]).astype(jnp.int32)
    earlier = jnp.cumsum(onehot, axis=0) - onehot
    slot_rank = jnp.sum(earlier * onehot, axis=1)
    position = flat_ids * slot_count + slot_rank
    picker = (jnp.arange(experts_all * slot_count)[:, None] == position[None, :]).astype(jnp.int32)
    select = jnp.sum(picker.reshape(experts_all * slot_count, tok_rows, -1), axis=2).astype(
        jnp.bfloat16
    )
    outgoing = jnp.dot(select, normed, preferred_element_type=jnp.float32).astype(jnp.bfloat16)
    outgoing = outgoing.reshape(experts_all, slot_count, model_width)
    gate_weight = w_gate[0]
    up_weight = w_up[0]
    down_weight = w_down[0]
    produced = expert_block(
        lax.all_to_all(outgoing, ("pool", "dev"), split_axis=0, concat_axis=0, tiled=True),
        gate_weight,
        up_weight,
        down_weight,
    )
    returned = lax.all_to_all(produced, ("pool", "dev"), split_axis=0, concat_axis=0, tiled=True)
    returned = returned.reshape(experts_all * slot_count, model_width)
    gathered = returned[position].astype(jnp.float32).reshape(tok_rows, -1, model_width)
    mixture = jnp.sum(weights[:, :, None] * gathered, axis=1)
    return (resid_f + mixture).astype(jnp.bfloat16)


def solution(mesh):
    placed = (
        P(("pool", "dev"), None),
        P(("pool", "dev"), None),
        P(("pool", "dev"), None, None),
        P(("pool", "dev"), None, None),
        P("dev", None),
        P(),
        P(),
        P(("pool", "dev"), None, None),
        P(("pool", "dev"), None, None),
        P(("pool", "dev"), None, None),
        P(("pool", "dev"), None),
    )
    return jax.shard_map(
        shards, mesh=mesh, in_specs=placed, out_specs=P(("pool", "dev"), None), check_vma=False
    )
```

```python
import functools
import math

import jax
import jax.numpy as jnp
from jax import lax
from jax.experimental import pallas as pl
from jax.experimental.pallas import tpu as pltpu
from jax.sharding import PartitionSpec as P

MESH = pl.DeviceIdType.MESH
F32 = jnp.float32
BF16 = jnp.bfloat16

TOK = 16
D = 4096
HD = 128
KVH = 4
CTX = 128
HID = 768
EXPERTS = 128
STRIDE = (16, 4, 1)
START = (0, 1408, 2816)
WIDE = (1408, 1408, 1280)
ROT = tuple((r, (r + 1) % 3, (r + 2) % 3) for r in range(3))
ALL = 256


def iota(shape, dim):
    return lax.broadcasted_iota(jnp.int32, shape, dim)


def one_hot(mask):
    return jnp.where(mask, 1.0, 0.0).astype(BF16)


def dot(a, b):
    return jnp.dot(a, b, preferred_element_type=F32)


def dot_nt(a, b):
    return lax.dot_general(a, b, (((1,), (1,)), ((), ())), preferred_element_type=F32)


class Sems:
    def __init__(self, send, recv):
        self.send, self.recv, self.used = send, recv, 0

    def copy(self, src, dst, device):
        i = self.used
        self.used += 1
        return pltpu.make_async_remote_copy(
            src_ref=src,
            dst_ref=dst,
            send_sem=self.send.at[i],
            recv_sem=self.recv.at[i],
            device_id=device,
            device_id_type=MESH,
        )


N_COPIES = 9 + 9 + 45 + 18 + 36 + 42 + 18


def kernel(
    hidden_ref,
    query_ref,
    gain_ref,
    router_ref,
    routes_ref,
    key_hbm,
    value_hbm,
    ow_hbm,
    gate_hbm,
    up_hbm,
    down_hbm,
    out_ref,
    key_ref,
    value_ref,
    gate_ref,
    up_ref,
    down_ref,
    att,
    resid,
    normed,
    gate_acc,
    up_acc,
    *rest,
):
    rest = list(rest)

    def three():
        taken = rest[:3]
        del rest[:3]
        return taken

    weight, att_in, part1, over_b1, sum1, over_a1 = [three() for _ in range(6)]
    plane, plane_w, picked, rows, made, back = [three() for _ in range(6)]
    part2, over_b2, sum2, over_a2 = [three() for _ in range(4)]
    send, recv, local = rest
    sems = Sems(send, recv)

    pool = lax.axis_index("pool")
    dev = lax.axis_index("dev")
    at = (dev // 16, (dev // 4) % 4, dev % 4)

    def moved(*steps, other=0):
        where = list(at)
        for axis, step in steps:
            where[axis] = lax.rem(at[axis] + step, 4)
        there = where[0] * 16 + where[1] * 4 + where[2]
        return (lax.rem(pool + other, 2), there)

    def plus(axis, step):
        return lax.rem(at[axis] + step, 4)

    loads = []

    def load(src, dst):
        copy = pltpu.make_async_copy(src, dst, local.at[len(loads)])
        copy.start()
        loads.append(copy)
        return copy

    kv_loads = [load(key_hbm, key_ref), load(value_hbm, value_ref)]
    ow_loads = [
        load(ow_hbm.at[:, pl.ds(START[r], WIDE[r])], weight[r].at[at[ROT[r][0]]]) for r in range(3)
    ]
    expert_loads = [
        load(gate_hbm.at[0], gate_ref),
        load(up_hbm.at[0], up_ref),
        load(down_hbm.at[0], down_ref),
    ]

    barrier = pltpu.get_barrier_semaphore()
    partners = []
    for i in range(1, 64):
        steps = (i // 16, (i // 4) % 4, i % 4)
        moving = [(axis, step) for axis, step in enumerate(steps) if step]
        if len(moving) < 3:
            partners.append(moved(*moving))
    for axis in range(3):
        for step in range(1, 4):
            partners.append(moved((axis, step), other=1))
    partners.append(moved(other=1))
    for partner in partners:
        pl.semaphore_signal(barrier, inc=1, device_id=partner, device_id_type=MESH)
    pl.semaphore_wait(barrier, len(partners))

    half = pl.ds(pl.multiple_of(pool * 64, 64), 64)
    weight_out = []
    for r, (c, a, b) in enumerate(ROT):
        ow_loads[r].wait()
        mine = weight[r].at[at[c], half]
        for step in range(1, 4):
            copy = sems.copy(mine, mine, moved((c, step)))
            copy.start()
            weight_out.append(copy)

    for copy in kv_loads:
        copy.wait()
    row, col = iota((ALL, ALL), 0), iota((ALL, ALL), 1)
    swap = one_hot((row % TOK == col // TOK) & (row // TOK == col % TOK))
    for g in range(KVH):
        by_head = jnp.concatenate(
            [query_ref[:, pl.ds((g * TOK + h) * HD, HD)] for h in range(TOK)], axis=0
        )
        by_token = dot(swap, by_head).astype(BF16)
        lanes = pl.ds(g * HD, HD)
        scores = jnp.concatenate(
            [
                dot_nt(by_token[t * TOK : (t + 1) * TOK], key_ref[t, :, lanes])
                for t in range(TOK)
            ],
            axis=0,
        ) * (1.0 / math.sqrt(HD))
        top = jnp.max(scores, axis=-1, keepdims=True)
        raised = jnp.exp(scores - top)
        probs = (raised / jnp.sum(raised, axis=-1, keepdims=True)).astype(BF16)
        attended = jnp.concatenate(
            [dot(probs[t * TOK : (t + 1) * TOK], value_ref[t, :, lanes]) for t in range(TOK)],
            axis=0,
        ).astype(BF16)
        att[g] = dot(swap, attended).astype(BF16).reshape(4, 4, TOK, HD)

    att_out = []
    for r, (c, a, b) in enumerate(ROT):
        sent = []
        for step in range(16):
            step_b, step_a = step // 4, step % 4
            where = [None] * 3
            where[c] = pl.ds(0, 4)
            where[a], where[b] = plus(a, step_a), plus(b, step_b)
            src, dst = att.at[tuple(where)], att_in[r].at[at[b], at[a]]
            if step:
                copy = sems.copy(src, dst, moved((a, step_a), (b, step_b)))
                copy.start()
                sent.append(copy)
            else:
                own = pltpu.make_async_copy(src, dst, local.at[8 + r])
                own.start()
                sent.append(own)
        att_out.append(sent)

    twin_out = []
    for r, (c, a, b) in enumerate(ROT):
        for step in range(1, 4):
            weight_out[r * 3 + step - 1].wait_recv()
            held = weight[r].at[plus(c, 4 - step), half]
            copy = sems.copy(held, held, moved(other=1))
            copy.start()
            twin_out.append(copy)

    def scatter_b(r, part, over_b):
        c, a, b = ROT[r]
        sent = []
        for step in range(1, 4):
            copy = sems.copy(
                part[r].at[plus(b, step)], over_b[r].at[step - 1], moved((b, step))
            )
            copy.start()
            sent.append(copy)
        return sent

    def scatter_a(r, sent, part, over_b, summed, over_a):
        c, a, b = ROT[r]
        for copy in sent:
            copy.wait_recv()
        total = part[r][at[b]].astype(F32)
        for step in range(3):
            total = total + over_b[r][step].astype(F32)
        summed[r][...] = total.astype(BF16)
        out = []
        for step in range(1, 4):
            copy = sems.copy(
                summed[r].at[plus(a, step)], over_a[r].at[step - 1], moved((a, step))
            )
            copy.start()
            out.append(copy)
        return out

    def scattered(r, sent, summed, over_a):
        c, a, b = ROT[r]
        for copy in sent:
            copy.wait_recv()
        total = summed[r][at[a]].astype(F32)
        for step in range(3):
            total = total + over_a[r][step].astype(F32)
        return total

    b_out1 = []
    for r in range(3):
        for copy in twin_out[r * 3 : r * 3 + 3]:
            copy.wait_recv()
        for copy in att_out[r][1:]:
            copy.wait_recv()
        att_out[r][0].wait()
        held = att_in[r][...]
        lhs = jnp.concatenate(
            [held[:, :, c].reshape(ALL, HD) for c in range(4)], axis=1
        )
        rhs = weight[r][...].reshape(4 * HD, WIDE[r])
        part1[r][...] = dot(lhs, rhs).astype(BF16).reshape(4, 4, TOK, WIDE[r])
        b_out1.append(scatter_b(r, part1, over_b1))
    a_out1 = [scatter_a(r, b_out1[r], part1, over_b1, sum1, over_a1) for r in range(3)]
    square = jnp.zeros((TOK, 1), F32)
    for r in range(3):
        cols = pl.ds(START[r], WIDE[r])
        project = scattered(r, a_out1[r], sum1, over_a1)
        held = (hidden_ref[:, cols].astype(F32) + project).astype(BF16)
        resid[:, cols] = held
        held = held.astype(F32)
        square = square + jnp.sum(held * held, axis=-1, keepdims=True)
    scale = lax.rsqrt(square * (1.0 / D) + 1e-06)

    rows_a = []
    for r, (c, a, b) in enumerate(ROT):
        cols = pl.ds(START[r], WIDE[r])
        held = resid[:, cols].astype(F32) * scale * gain_ref[:, cols].astype(F32)
        held = held.astype(BF16)
        normed[:, cols] = held
        plane[r][at[b], at[a]] = held
        mine = plane[r].at[at[b], at[a]]
        sent = []
        for step in range(1, 4):
            copy = sems.copy(mine, mine, moved((a, step)))
            copy.start()
            sent.append(copy)
        rows_a.append(sent)

    logits = dot(normed[...], router_ref[...])
    ids = iota((TOK, EXPERTS), 1)
    routes = routes_ref[...]
    chosen = routes[:, 0:1] == ids
    for k in range(1, routes.shape[1]):
        chosen = chosen | (routes[:, k : k + 1] == ids)
    top = jnp.max(jnp.where(chosen, logits, -jnp.inf), axis=-1, keepdims=True)
    raised = jnp.where(chosen, jnp.exp(jnp.where(chosen, logits, top) - top), 0.0)
    shares = (raised / jnp.sum(raised, axis=-1, keepdims=True)).astype(BF16)
    shares_a = []
    for r, (c, a, b) in enumerate(ROT):
        plane_w[r][at[b], at[a]] = shares
        mine = plane_w[r].at[at[b], at[a]]
        sent = []
        for step in range(1, 4):
            copy = sems.copy(mine, mine, moved((a, step)))
            copy.start()
            sent.append(copy)
        shares_a.append(sent)

    rows_b, shares_b = [], []
    for r, (c, a, b) in enumerate(ROT):
        for held, before, after in (
            (plane_w[r], shares_a[r], shares_b),
            (plane[r], rows_a[r], rows_b),
        ):
            for copy in before:
                copy.wait_recv()
            sent = []
            for step in range(1, 4):
                copy = sems.copy(held.at[at[b]], held.at[at[b]], moved((b, step)))
                copy.start()
                sent.append(copy)
            after.append(sent)

    same = row // TOK == col // TOK
    line_out, combine = [], []
    for r, (c, a, b) in enumerate(ROT):
        for copy in shares_b[r]:
            copy.wait_recv()
        own = at[a] * STRIDE[a] + at[b] * STRIDE[b]

        def expert(slot):
            return slot // 64 * STRIDE[c] + slot // 32 % 2 * 64 + own

        held = plane_w[r][...].reshape(ALL, EXPERTS)
        names = one_hot(expert(iota((ALL, EXPERTS), 0)) == iota((ALL, EXPERTS), 1))
        share = dot_nt(names, held)
        uses = share > 0
        rank = dot(one_hot(uses), one_hot(same & (row < col)))
        uses = uses & (rank == (row % 2).astype(F32)) & (row // 2 % 16 == col // TOK)
        select = one_hot(uses)
        share = dot_nt(held, names)
        uses = share > 0
        rank = dot(one_hot(same & (col < row)), one_hot(uses))
        uses = uses & (rank == (col % 2).astype(F32)) & (col // 2 % 16 == row // TOK)
        combine.append(jnp.where(uses, share, 0.0).astype(BF16))
        for copy in rows_b[r]:
            copy.wait_recv()
        outgoing = dot(select, plane[r][...].reshape(ALL, WIDE[r])).astype(BF16)
        picked[r][...] = outgoing.reshape(4, 2, 32, WIDE[r])
        sent = []
        for step in range(1, 8):
            step_p, step_c = step // 4, step % 4
            copy = sems.copy(
                picked[r].at[plus(c, step_c), lax.rem(pool + step_p, 2)],
                rows[r].at[at[c], pool],
                moved((c, step_c), other=step_p),
            )
            copy.start()
            sent.append(copy)
        rows[r][at[c], pool] = picked[r][at[c], pool]
        line_out.append(sent)

    for copy in expert_loads:
        copy.wait()

    def place(slot, r):
        rank = slot % 2
        coord = {0: slot // 64, 2: slot // 8 % 4, 1: slot // 2 % 4}
        core = slot // 32 % 2
        c, a, b = ROT[r]
        return coord[c] * 64 + core * 32 + coord[b] * 8 + coord[a] * 2 + rank

    for r in range(3):
        for copy in line_out[r]:
            copy.wait_recv()
        held = rows[r][...].reshape(ALL, WIDE[r])
        if r:
            held = dot(one_hot(place(row, r) == col), held).astype(BF16)
        cols = pl.ds(START[r], WIDE[r])
        gate = dot(held, gate_ref[cols, :])
        up = dot(held, up_ref[cols, :])
        if r:
            gate, up = gate_acc[...] + gate, up_acc[...] + up
        gate_acc[...] = gate
        up_acc[...] = up
    gate = gate_acc[...]
    activated = (gate / (1.0 + jnp.exp(-gate)) * up_acc[...]).astype(BF16)
    line_back = []
    for r, (c, a, b) in enumerate(ROT):
        held = activated
        if r:
            held = dot(one_hot(place(col, r) == row), held).astype(BF16)
        result = dot(held, down_ref[:, pl.ds(START[r], WIDE[r])]).astype(BF16)
        made[r][...] = result.reshape(4, 2, 32, WIDE[r])
        sent = []
        for step in range(1, 8):
            step_p, step_c = step // 4, step % 4
            copy = sems.copy(
                made[r].at[plus(c, step_c), lax.rem(pool + step_p, 2)],
                back[r].at[at[c], pool],
                moved((c, step_c), other=step_p),
            )
            copy.start()
            sent.append(copy)
        back[r][at[c], pool] = made[r][at[c], pool]
        line_back.append(sent)

    b_out2 = []
    for r in range(3):
        for copy in line_back[r]:
            copy.wait_recv()
        total = dot(combine[r], back[r][...].reshape(ALL, WIDE[r]))
        part2[r][...] = total.astype(BF16).reshape(4, 4, TOK, WIDE[r])
        b_out2.append(scatter_b(r, part2, over_b2))
    a_out2 = [scatter_a(r, b_out2[r], part2, over_b2, sum2, over_a2) for r in range(3)]
    for r in range(3):
        cols = pl.ds(START[r], WIDE[r])
        mixture = scattered(r, a_out2[r], sum2, over_a2)
        out_ref[:, cols] = (resid[:, cols].astype(F32) + mixture).astype(BF16)

    sent = weight_out + twin_out
    for group in (b_out1, a_out1, rows_a, shares_a, rows_b, shares_b, line_out, line_back, b_out2, a_out2):
        for copies in group:
            sent += copies
    for copies in att_out:
        sent += copies[1:]
    for copy in sent:
        copy.wait_send()


def shards(hidden, queries, k_cache, v_cache, o_weight, norm_gain, router_weight, w_gate, w_up, w_down, routes):
    vmem, hbm = pl.BlockSpec(memory_space=pltpu.VMEM), pl.BlockSpec(memory_space=pl.ANY)

    def three(*lead, cols=None):
        return [pltpu.VMEM((*lead, cols or wide), BF16) for wide in WIDE]

    scratch = [
        pltpu.VMEM((TOK, CTX, KVH * HD), BF16),
        pltpu.VMEM((TOK, CTX, KVH * HD), BF16),
        pltpu.VMEM((D, HID), BF16),
        pltpu.VMEM((D, HID), BF16),
        pltpu.VMEM((HID, D), BF16),
        pltpu.VMEM((4, 4, 4, TOK, HD), BF16),
        pltpu.VMEM((TOK, D), BF16),
        pltpu.VMEM((TOK, D), BF16),
        pltpu.VMEM((ALL, HID), F32),
        pltpu.VMEM((ALL, HID), F32),
        *three(4, HD),
        *three(4, 4, 4, TOK, cols=HD),
        *three(4, 4, TOK),
        *three(3, 4, TOK),
        *three(4, TOK),
        *three(3, TOK),
        *three(4, 4, TOK),
        *three(4, 4, TOK, cols=EXPERTS),
        *three(4, 2, 32),
        *three(4, 2, 32),
        *three(4, 2, 32),
        *three(4, 2, 32),
        *three(4, 4, TOK),
        *three(3, 4, TOK),
        *three(4, TOK),
        *three(3, TOK),
        pltpu.SemaphoreType.DMA((N_COPIES,)),
        pltpu.SemaphoreType.DMA((N_COPIES,)),
        pltpu.SemaphoreType.DMA((11,)),
    ]
    return pl.pallas_call(
        kernel,
        out_shape=jax.ShapeDtypeStruct((TOK, D), BF16),
        in_specs=[vmem] * 5 + [hbm] * 6,
        out_specs=vmem,
        scratch_shapes=scratch,
        compiler_params=pltpu.CompilerParams(
            collective_id=0, has_side_effects=True, vmem_limit_bytes=60 * 1024 * 1024
        ),
    )(
        hidden,
        queries,
        norm_gain.reshape(1, D),
        router_weight,
        routes,
        k_cache,
        v_cache,
        o_weight,
        w_gate,
        w_up,
        w_down,
    )


def solution(mesh):
    rows = P(("pool", "dev"), None)
    cube = P(("pool", "dev"), None, None)
    placed = (rows, rows, cube, cube, P("dev", None), P(), P(), cube, cube, cube, rows)
    return jax.shard_map(shards, mesh=mesh, in_specs=placed, out_specs=rows, check_vma=False)
```

```python
import functools
import math

import jax
import jax.numpy as jnp
from jax import lax
from jax.experimental import pallas as pl
from jax.experimental.pallas import tpu as pltpu
from jax.sharding import PartitionSpec as P

MESH = pl.DeviceIdType.MESH
F32 = jnp.float32
BF16 = jnp.bfloat16

TOK = 16
D = 4096
HD = 128
KVH = 4
CTX = 128
HID = 768
EXPERTS = 128
STRIDE = (16, 4, 1)
START = (0, 512, 1024, 1536, 2048, 2560, 2944, 3328, 3712)
WIDE = (512, 512, 512, 512, 512, 384, 384, 384, 384)
PARTS = len(WIDE)
ROT = tuple((p % 3, (p + 1) % 3, (p + 2) % 3) for p in range(PARTS))
NEAR_FIRST = (1, 3, 2)
ALL = 256


def iota(shape, dim):
    return lax.broadcasted_iota(jnp.int32, shape, dim)


def one_hot(mask):
    return jnp.where(mask, 1.0, 0.0).astype(BF16)


def dot(a, b):
    return jnp.dot(a, b, preferred_element_type=F32)


def dot_nt(a, b):
    return lax.dot_general(a, b, (((1,), (1,)), ((), ())), preferred_element_type=F32)


class Group:
    def __init__(self, sems, like):
        self.send, self.recv = sems
        self.like = like

    def push(self, src, dst, device):
        pltpu.make_async_remote_copy(
            src_ref=src,
            dst_ref=dst,
            send_sem=self.send,
            recv_sem=self.recv,
            device_id=device,
            device_id_type=MESH,
        ).start()

    def arrived(self):
        pltpu.make_async_copy(self.like, self.like, self.recv).wait()

    def sent(self):
        pltpu.make_async_copy(self.like, self.like, self.send).wait()


N_GROUPS = 11 * PARTS + 11
N_LOADS = 9


def kernel(
    gain_ref,
    routes_ref,
    hidden_hbm,
    query_hbm,
    router_hbm,
    key_hbm,
    value_hbm,
    ow_hbm,
    gate_hbm,
    up_hbm,
    down_hbm,
    out_ref,
    hidden_ref,
    query_ref,
    router_ref,
    key_ref,
    value_ref,
    gate_ref,
    up_ref,
    down_ref,
    ow_ref,
    att,
    mid_x,
    mid_z,
    resid,
    normed,
    gate_acc,
    up_acc,
    *rest,
):
    rest = list(rest)

    def take(count):
        taken = rest[:count]
        del rest[:count]
        return taken

    att_in, plane_w = take(3), take(3)
    weight, part1, over_b1, sum1, over_a1 = [take(PARTS) for _ in range(5)]
    plane, picked, rows, made, back = [take(PARTS) for _ in range(5)]
    part2, over_b2, sum2, over_a2 = [take(PARTS) for _ in range(4)]
    send, recv, local = rest
    groups = []

    def group(like):
        i = len(groups)
        groups.append(Group((send.at[i], recv.at[i]), like))
        return groups[i]


    pool = lax.axis_index("pool")
    dev = lax.axis_index("dev")
    at = (dev // 16, (dev // 4) % 4, dev % 4)

    def moved(*steps, other=0):
        where = list(at)
        for axis, step in steps:
            where[axis] = lax.rem(at[axis] + step, 4)
        there = where[0] * 16 + where[1] * 4 + where[2]
        return (lax.rem(pool + other, 2), there)

    def plus(axis, step):
        return lax.rem(at[axis] + step, 4)

    def drain(*copies):
        for copy in copies:
            copy.sent()

    barrier = pltpu.get_barrier_semaphore()
    partners = [moved(other=1)]
    for axis in range(3):
        for step in range(1, 4):
            partners += [moved((axis, step)), moved((axis, step), other=1)]
    for partner in partners:
        pl.semaphore_signal(barrier, inc=1, device_id=partner, device_id_type=MESH)

    loads = []

    def load(src, dst):
        copy = pltpu.make_async_copy(src, dst, local.at[len(loads)])
        copy.start()
        loads.append(copy)
        return copy

    ow_load, query_load, key_load, value_load = [
        load(src, dst)
        for src, dst in (
            (ow_hbm, ow_ref),
            (query_hbm, query_ref),
            (key_hbm, key_ref),
            (value_hbm, value_ref),
        )
    ]

    row, col = iota((ALL, ALL), 0), iota((ALL, ALL), 1)
    swap = one_hot((row % TOK == col // TOK) & (row // TOK == col % TOK))

    def attend():
        empty = jnp.zeros((TOK, HD), BF16)
        asked = []
        for g in range(KVH):
            by_head = jnp.concatenate(
                [query_ref[:, (g * TOK + h) * HD : (g * TOK + h + 1) * HD] for h in range(TOK)],
                axis=0,
            )
            asked.append(dot(swap, by_head).astype(BF16))
        scores = []
        for t in range(TOK):
            rows = [
                jnp.concatenate(
                    [asked[g][t * TOK : (t + 1) * TOK] if g == i else empty for i in range(KVH)],
                    axis=1,
                )
                for g in range(KVH)
            ]
            scores.append(dot_nt(jnp.concatenate(rows, axis=0), key_ref[t]))
        scores = jnp.concatenate(scores, axis=0) * (1.0 / math.sqrt(HD))
        top = jnp.max(scores, axis=-1, keepdims=True)
        raised = jnp.exp(scores - top)
        probs = (raised / jnp.sum(raised, axis=-1, keepdims=True)).astype(BF16)
        wide = KVH * TOK
        found = [dot(probs[t * wide : (t + 1) * wide], value_ref[t]) for t in range(TOK)]
        for g in range(KVH):
            rows, lanes = slice(g * TOK, (g + 1) * TOK), slice(g * HD, (g + 1) * HD)
            attended = jnp.concatenate([held[rows, lanes] for held in found], axis=0)
            att[g] = dot(swap, attended.astype(BF16)).astype(BF16).reshape(4, 4, TOK, HD)

    half = pl.ds(pl.multiple_of(pool * 64, 64), 64)
    quarters = [pl.ds(pl.multiple_of(pool * 64 + i, 32), 32) for i in (0, 32)]
    weight_near, weight_far, twin = [], [], []

    def send_weight(p):
        c, a, b = ROT[p]
        cols = pl.ds(START[p], WIDE[p])
        src, dst = ow_ref.at[half, cols], weight[p].at[at[c], half]
        copies = group(weight[p].at[0])
        for hop in (1, 3):
            copies.push(src, dst, moved((c, hop)))
        weight_near.append(copies)
        weight[p][at[c]] = ow_ref[:, cols]

    def pass_weight(p):
        c, a, b = ROT[p]
        weight_near[p].arrived()
        copies = group(weight[p].at[0, 0:64])
        for hop, rows in ((1, quarters[0]), (3, quarters[1])):
            held = weight[p].at[plus(c, 4 - hop), rows]
            copies.push(held, held, moved((c, hop)))
        weight_far.append(copies)
        copies = group(weight[p].at[0:3, 0:64])
        for hop in (1, 3):
            held = weight[p].at[plus(c, hop), half]
            copies.push(held, held, moved(other=1))
        twin.append(copies)

    def hand_over(p):
        c, a, b = ROT[p]
        weight_far[p].arrived()
        held = weight[p].at[plus(c, 2), half]
        twin[p].push(held, held, moved(other=1))

    query_load.wait()
    key_load.wait()
    value_load.wait()
    attend()
    pl.semaphore_wait(barrier, len(partners))
    over_x, over_z = group(mid_x.at[0:3]), group(mid_z.at[0:3])
    for hop in NEAR_FIRST:
        over_x.push(att.at[plus(0, hop)], mid_x.at[at[0]], moved((0, hop)))
        over_z.push(att.at[:, plus(1, hop)], mid_z.at[at[1]], moved((1, hop)))
    ow_load.wait()
    for p in range(PARTS):
        send_weight(p)
    mid_x[at[0]] = att[at[0]]
    mid_z[at[1]] = att[:, at[1]]
    att_out = [group(att_in[r].at[0:3]) for r in range(3)]
    over_x.arrived()
    for hop in NEAR_FIRST:
        att_out[2].push(mid_x.at[:, plus(1, hop)], att_in[2].at[at[1]], moved((1, hop)))
        att_out[1].push(mid_x.at[:, :, plus(2, hop)], att_in[1].at[:, at[2]], moved((2, hop)))
    over_z.arrived()
    for hop in NEAR_FIRST:
        att_out[0].push(mid_z.at[:, :, plus(2, hop)], att_in[0].at[at[2]], moved((2, hop)))
    att_in[2][at[1]] = mid_x[:, at[1]]
    att_in[1][:, at[2]] = mid_x[:, :, at[2]]
    att_in[0][at[2]] = mid_z[:, :, at[2]]
    for p in range(PARTS):
        pass_weight(p)
    for p in range(PARTS):
        hand_over(p)
    small_loads = [load(hidden_hbm, hidden_ref), load(router_hbm, router_ref)]
    expert_loads = [
        load(gate_hbm.at[0], gate_ref),
        load(up_hbm.at[0], up_ref),
        load(down_hbm.at[0], down_ref),
    ]

    def scatter_b(p, part, over_b):
        c, a, b = ROT[p]
        copies = group(over_b[p])
        for hop in NEAR_FIRST:
            copies.push(part[p].at[plus(b, hop)], over_b[p].at[hop - 1], moved((b, hop)))
        return copies

    def scatter_a(p, before, part, over_b, summed, over_a):
        c, a, b = ROT[p]
        before.arrived()
        total = part[p][at[b]].astype(F32)
        for i in range(3):
            total = total + over_b[p][i].astype(F32)
        summed[p][...] = total.astype(BF16)
        copies = group(over_a[p])
        for hop in NEAR_FIRST:
            copies.push(summed[p].at[plus(a, hop)], over_a[p].at[hop - 1], moved((a, hop)))
        return copies

    def scattered(p, copies, summed, over_a):
        c, a, b = ROT[p]
        copies.arrived()
        total = summed[p][at[a]].astype(F32)
        for i in range(3):
            total = total + over_a[p][i].astype(F32)
        return total

    b_out1 = []
    lhs = []
    for p in range(PARTS):
        if p < 3:
            att_out[p].arrived()
            held = att_in[p][...]
            lhs.append(
                jnp.concatenate([held[:, :, i].reshape(ALL, HD) for i in range(4)], axis=1)
            )
        twin[p].arrived()
        rhs = weight[p][...].reshape(4 * HD, WIDE[p])
        part1[p][...] = dot(lhs[p % 3], rhs).astype(BF16).reshape(4, 4, TOK, WIDE[p])
        b_out1.append(scatter_b(p, part1, over_b1))
    drain(over_x, over_z, *weight_near, *weight_far, *twin)

    squares = []
    rows_a = []
    a_out1 = [scatter_a(p, b_out1[p], part1, over_b1, sum1, over_a1) for p in range(PARTS)]

    def finish(p):
        c, a, b = ROT[p]
        cols = pl.ds(START[p], WIDE[p])
        held = (hidden_ref[:, cols].astype(F32) + scattered(p, a_out1[p], sum1, over_a1)).astype(
            BF16
        )
        resid[:, cols] = held
        plane[p][at[b], at[a]] = held
        mine = plane[p].at[at[b], at[a]]
        copies = group(plane[p].at[0, 0:3])
        for hop in NEAR_FIRST:
            copies.push(mine, mine, moved((a, hop)))
        rows_a.append(copies)
        held = held.astype(F32)
        squares.append(jnp.sum(held * held, axis=-1, keepdims=True))

    def gather_b(p):
        c, a, b = ROT[p]
        rows_a[p].arrived()
        mine = plane[p].at[at[b]]
        copies = group(plane[p].at[0:3])
        for hop in NEAR_FIRST:
            copies.push(mine, mine, moved((b, hop)))
        return copies

    for copy in small_loads:
        copy.wait()
    for p in range(PARTS):
        finish(p)
    rows_b = [gather_b(p) for p in range(3)]
    scale = lax.rsqrt(sum(squares) * (1.0 / D) + 1e-06)

    def norm(held, scale, i):
        held = held.astype(F32) * scale * gain_ref[i // 128 : i // 128 + 1, :].astype(F32)
        return held.astype(BF16)

    for i in range(0, D, 128):
        normed[:, i : i + 128] = norm(resid[:, i : i + 128], scale, i)

    logits = dot(normed[...], router_ref[...])
    ids = iota((TOK, EXPERTS), 1)
    eye = one_hot(iota((TOK, TOK), 0) == iota((TOK, TOK), 1))
    routes = dot_nt(eye, routes_ref[...].astype(F32).astype(BF16)).astype(jnp.int32)
    chosen = routes[:, 0:1] == ids
    for k in range(1, routes.shape[1]):
        chosen = chosen | (routes[:, k : k + 1] == ids)
    top = jnp.max(jnp.where(chosen, logits, -jnp.inf), axis=-1, keepdims=True)
    raised = jnp.where(chosen, jnp.exp(jnp.where(chosen, logits, top) - top), 0.0)
    shares = (raised / jnp.sum(raised, axis=-1, keepdims=True)).astype(BF16)
    lane = iota((TOK, EXPERTS), 1)
    high = scale.astype(BF16).astype(F32)
    middle = (scale - high).astype(BF16).astype(F32)
    low = scale - high - middle
    scales = jnp.where(lane == 0, high, jnp.where(lane == 1, middle, jnp.where(lane == 2, low, 0.0)))
    shares_a = []
    for r in range(3):
        c, a, b = ROT[r]
        plane_w[r][at[b], at[a], :, 0:EXPERTS] = shares
        plane_w[r][at[b], at[a], :, EXPERTS : 2 * EXPERTS] = scales.astype(BF16)
        mine = plane_w[r].at[at[b], at[a]]
        copies = group(plane_w[r].at[0, 0:3])
        for hop in NEAR_FIRST:
            copies.push(mine, mine, moved((a, hop)))
        shares_a.append(copies)

    rows_b += [gather_b(p) for p in range(3, PARTS)]
    shares_b = []
    for r in range(3):
        c, a, b = ROT[r]
        shares_a[r].arrived()
        mine = plane_w[r].at[at[b]]
        copies = group(plane_w[r].at[0:3])
        for hop in NEAR_FIRST:
            copies.push(mine, mine, moved((b, hop)))
        shares_b.append(copies)
    drain(*att_out, *b_out1, *a_out1, *rows_a, *shares_a)

    same = row // TOK == col // TOK
    select, combine, scales = [], [], []
    for r in range(3):
        c, a, b = ROT[r]
        shares_b[r].arrived()
        own = at[a] * STRIDE[a] + at[b] * STRIDE[b]

        def expert(slot):
            return slot // 64 * STRIDE[c] + slot // 32 % 2 * 64 + own

        held = plane_w[r][...].reshape(ALL, 2 * EXPERTS)
        scales.append(jnp.sum(held[:, EXPERTS:].astype(F32), axis=-1, keepdims=True))
        held = held[:, :EXPERTS]
        names = one_hot(expert(iota((ALL, EXPERTS), 0)) == iota((ALL, EXPERTS), 1))
        share = dot_nt(names, held)
        uses = share > 0
        rank = dot(one_hot(uses), one_hot(same & (row < col)))
        uses = uses & (rank == (row % 2).astype(F32)) & (row // 2 % 16 == col // TOK)
        select.append(one_hot(uses))
        share = dot_nt(held, names)
        uses = share > 0
        rank = dot(one_hot(same & (col < row)), one_hot(uses))
        uses = uses & (rank == (col % 2).astype(F32)) & (col // 2 % 16 == row // TOK)
        combine.append(jnp.where(uses, share, 0.0).astype(BF16))

    def along_line(p, src, dst):
        c, a, b = ROT[p]
        copies = group(src[p].at[0:7])
        for step in (1, 3, 5, 7, 2, 6, 4):
            step_p, step_c = step // 4, step % 4
            there = plus(c, step_c) * 2 + lax.rem(pool + step_p, 2)
            copies.push(
                src[p].at[there], dst[p].at[at[c] * 2 + pool], moved((c, step_c), other=step_p)
            )
        dst[p][at[c] * 2 + pool] = src[p][at[c] * 2 + pool]
        return copies

    line_out = []
    for p in range(PARTS):
        rows_b[p].arrived()
        held = plane[p][...].reshape(ALL, WIDE[p])
        held = jnp.concatenate(
            [
                norm(held[:, i : i + 128], scales[p % 3], START[p] + i)
                for i in range(0, WIDE[p], 128)
            ],
            axis=1,
        )
        outgoing = dot(select[p % 3], held).astype(BF16)
        picked[p][...] = outgoing.reshape(8, 32, WIDE[p])
        line_out.append(along_line(p, picked, rows))
    drain(*rows_b, *shares_b)

    for copy in expert_loads:
        copy.wait()

    def place(slot, r):
        rank = slot % 2
        coord = {0: slot // 64, 2: slot // 8 % 4, 1: slot // 2 % 4}
        core = slot // 32 % 2
        c, a, b = ROT[r]
        return coord[c] * 64 + core * 32 + coord[b] * 8 + coord[a] * 2 + rank

    for p in range(PARTS):
        line_out[p].arrived()
        held = rows[p][...].reshape(ALL, WIDE[p])
        if p % 3:
            held = dot(one_hot(place(row, p % 3) == col), held).astype(BF16)
        cols = pl.ds(START[p], WIDE[p])
        gate = dot(held, gate_ref[cols, :])
        up = dot(held, up_ref[cols, :])
        if p:
            gate, up = gate_acc[...] + gate, up_acc[...] + up
        gate_acc[...] = gate
        up_acc[...] = up
    gate = gate_acc[...]
    activated = (gate / (1.0 + jnp.exp(-gate)) * up_acc[...]).astype(BF16)
    activated = [activated] + [
        dot(one_hot(place(col, r) == row), activated).astype(BF16) for r in (1, 2)
    ]
    line_back = []
    for p in range(PARTS):
        result = dot(activated[p % 3], down_ref[:, pl.ds(START[p], WIDE[p])]).astype(BF16)
        made[p][...] = result.reshape(8, 32, WIDE[p])
        line_back.append(along_line(p, made, back))
    drain(*line_out)

    b_out2 = []
    for p in range(PARTS):
        line_back[p].arrived()
        total = dot(combine[p % 3], back[p][...].reshape(ALL, WIDE[p]))
        part2[p][...] = total.astype(BF16).reshape(4, 4, TOK, WIDE[p])
        b_out2.append(scatter_b(p, part2, over_b2))
    drain(*line_back)
    a_out2 = [scatter_a(p, b_out2[p], part2, over_b2, sum2, over_a2) for p in range(PARTS)]
    drain(*b_out2)
    for p in range(PARTS):
        cols = pl.ds(START[p], WIDE[p])
        mixture = scattered(p, a_out2[p], sum2, over_a2)
        out_ref[:, cols] = (resid[:, cols].astype(F32) + mixture).astype(BF16)
    drain(*a_out2)


def shards(hidden, queries, k_cache, v_cache, o_weight, norm_gain, router_weight, w_gate, w_up, w_down, routes):
    vmem, hbm = pl.BlockSpec(memory_space=pltpu.VMEM), pl.BlockSpec(memory_space=pl.ANY)

    def parts(*lead):
        return [pltpu.VMEM((*lead, wide), BF16) for wide in WIDE]

    scratch = [
        pltpu.VMEM((TOK, D), BF16),
        pltpu.VMEM((TOK, 2 * D), BF16),
        pltpu.VMEM((D, EXPERTS), BF16),
        pltpu.VMEM((TOK, CTX, KVH * HD), BF16),
        pltpu.VMEM((TOK, CTX, KVH * HD), BF16),
        pltpu.VMEM((D, HID), BF16),
        pltpu.VMEM((D, HID), BF16),
        pltpu.VMEM((HID, D), BF16),
        pltpu.VMEM((HD, D), BF16),
        *[pltpu.VMEM((4, 4, 4, TOK, HD), BF16)] * 3,
        pltpu.VMEM((TOK, D), BF16),
        pltpu.VMEM((TOK, D), BF16),
        pltpu.VMEM((ALL, HID), F32),
        pltpu.VMEM((ALL, HID), F32),
        *[pltpu.VMEM((4, 4, 4, TOK, HD), BF16)] * 3,
        *[pltpu.VMEM((4, 4, TOK, 2 * EXPERTS), BF16)] * 3,
        *parts(4, HD),
        *parts(4, 4, TOK),
        *parts(3, 4, TOK),
        *parts(4, TOK),
        *parts(3, TOK),
        *parts(4, 4, TOK),
        *parts(8, 32),
        *parts(8, 32),
        *parts(8, 32),
        *parts(8, 32),
        *parts(4, 4, TOK),
        *parts(3, 4, TOK),
        *parts(4, TOK),
        *parts(3, TOK),
        pltpu.SemaphoreType.DMA((N_GROUPS,)),
        pltpu.SemaphoreType.DMA((N_GROUPS,)),
        pltpu.SemaphoreType.DMA((N_LOADS,)),
    ]
    return pl.pallas_call(
        kernel,
        out_shape=jax.ShapeDtypeStruct((TOK, D), BF16),
        in_specs=[vmem] * 2 + [hbm] * 9,
        out_specs=vmem,
        scratch_shapes=scratch,
        compiler_params=pltpu.CompilerParams(
            collective_id=0, has_side_effects=True, vmem_limit_bytes=60 * 1024 * 1024
        ),
    )(
        norm_gain.reshape(D // 128, 128),
        routes.T,
        hidden,
        queries,
        router_weight,
        k_cache,
        v_cache,
        o_weight,
        w_gate,
        w_up,
        w_down,
    )


def solution(mesh):
    rows = P(("pool", "dev"), None)
    cube = P(("pool", "dev"), None, None)
    placed = (rows, rows, cube, cube, P("dev", None), P(), P(), cube, cube, cube, rows)
    return jax.shard_map(shards, mesh=mesh, in_specs=placed, out_specs=rows, check_vma=False)
```

```python
import functools
import math

import jax
import jax.numpy as jnp
from jax import lax
from jax.experimental import pallas as pl
from jax.experimental.pallas import tpu as pltpu
from jax.sharding import PartitionSpec as P

MESH = pl.DeviceIdType.MESH
F32 = jnp.float32
BF16 = jnp.bfloat16

TOK = 16
D = 4096
HD = 128
KVH = 4
CTX = 128
HID = 768
EXPERTS = 128
STRIDE = (16, 4, 1)
START = (0, 512, 1024, 1536, 2048, 2560, 2944, 3328, 3712)
WIDE = (512, 512, 512, 512, 512, 384, 384, 384, 384)
PARTS = len(WIDE)
ROT = tuple((p % 3, (p + 1) % 3, (p + 2) % 3) for p in range(PARTS))
NEAR_FIRST = (1, 3, 2)
ALL = 256


def iota(shape, dim):
    return lax.broadcasted_iota(jnp.int32, shape, dim)


def one_hot(mask):
    return jnp.where(mask, 1.0, 0.0).astype(BF16)


def dot(a, b):
    return jnp.dot(a, b, preferred_element_type=F32)


def dot_nt(a, b):
    return lax.dot_general(a, b, (((1,), (1,)), ((), ())), preferred_element_type=F32)


class Group:
    def __init__(self, sems, like):
        self.send, self.recv = sems
        self.like = like

    def push(self, src, dst, device):
        pltpu.make_async_remote_copy(
            src_ref=src,
            dst_ref=dst,
            send_sem=self.send,
            recv_sem=self.recv,
            device_id=device,
            device_id_type=MESH,
        ).start()

    def arrived(self):
        pltpu.make_async_copy(self.like, self.like, self.recv).wait()

    def sent(self):
        pltpu.make_async_copy(self.like, self.like, self.send).wait()


N_GROUPS = 10 * PARTS + 18
N_LOADS = 9


def kernel(
    gain_ref,
    routes_ref,
    hidden_hbm,
    query_hbm,
    router_hbm,
    key_hbm,
    value_hbm,
    ow_hbm,
    gate_hbm,
    up_hbm,
    down_hbm,
    out_ref,
    hidden_ref,
    query_ref,
    router_ref,
    key_ref,
    value_ref,
    gate_ref,
    up_ref,
    down_ref,
    ow_ref,
    att,
    mid_x,
    mid_z,
    resid,
    normed,
    gate_acc,
    up_acc,
    *rest,
):
    rest = list(rest)

    def take(count):
        taken = rest[:count]
        del rest[:count]
        return taken

    att_in, plane_u, plane_w = take(3), take(3), take(3)
    scale_out, scale_in = take(2)
    weight, part1, over_b1, swap_a = [take(PARTS) for _ in range(4)]
    plane, picked, rows, made, back = [take(PARTS) for _ in range(5)]
    part2, over_b2, sum2, over_a2 = [take(PARTS) for _ in range(4)]
    send, recv, local = rest
    groups = []

    def group(like):
        i = len(groups)
        groups.append(Group((send.at[i], recv.at[i]), like))
        return groups[i]


    pool = lax.axis_index("pool")
    dev = lax.axis_index("dev")
    at = (dev // 16, (dev // 4) % 4, dev % 4)

    def moved(*steps, other=0):
        where = list(at)
        for axis, step in steps:
            where[axis] = lax.rem(at[axis] + step, 4)
        there = where[0] * 16 + where[1] * 4 + where[2]
        return (lax.rem(pool + other, 2), there)

    def plus(axis, step):
        return lax.rem(at[axis] + step, 4)

    def drain(*copies):
        for copy in copies:
            copy.sent()

    loads = []

    def load(src, dst):
        copy = pltpu.make_async_copy(src, dst, local.at[len(loads)])
        copy.start()
        loads.append(copy)
        return copy

    query_load, key_load, value_load, ow_load, hidden_load = [
        load(src, dst)
        for src, dst in (
            (query_hbm, query_ref),
            (key_hbm, key_ref),
            (value_hbm, value_ref),
            (ow_hbm, ow_ref),
            (hidden_hbm, hidden_ref),
        )
    ]

    barrier = pltpu.get_barrier_semaphore()
    partners = [moved(other=1)]
    for axis in range(3):
        for step in range(1, 4):
            partners += [moved((axis, step)), moved((axis, step), other=1)]
    for partner in partners:
        pl.semaphore_signal(barrier, inc=1, device_id=partner, device_id_type=MESH)

    row, col = iota((ALL, ALL), 0), iota((ALL, ALL), 1)
    swap = one_hot((row % TOK == col // TOK) & (row // TOK == col % TOK))

    def attend():
        empty = jnp.zeros((TOK, HD), BF16)
        asked = []
        for g in range(KVH):
            by_head = jnp.concatenate(
                [query_ref[:, (g * TOK + h) * HD : (g * TOK + h + 1) * HD] for h in range(TOK)],
                axis=0,
            )
            asked.append(dot(swap, by_head).astype(BF16))
        scores = []
        for t in range(TOK):
            rows = [
                jnp.concatenate(
                    [asked[g][t * TOK : (t + 1) * TOK] if g == i else empty for i in range(KVH)],
                    axis=1,
                )
                for g in range(KVH)
            ]
            scores.append(dot_nt(jnp.concatenate(rows, axis=0), key_ref[t]))
        scores = jnp.concatenate(scores, axis=0) * (1.0 / math.sqrt(HD))
        top = jnp.max(scores, axis=-1, keepdims=True)
        raised = jnp.exp(scores - top)
        probs = (raised / jnp.sum(raised, axis=-1, keepdims=True)).astype(BF16)
        wide = KVH * TOK
        found = [dot(probs[t * wide : (t + 1) * wide], value_ref[t]) for t in range(TOK)]
        for g in range(KVH):
            rows, lanes = slice(g * TOK, (g + 1) * TOK), slice(g * HD, (g + 1) * HD)
            attended = jnp.concatenate([held[rows, lanes] for held in found], axis=0)
            att[g] = dot(swap, attended.astype(BF16)).astype(BF16).reshape(4, 4, TOK, HD)

    half = pl.ds(pl.multiple_of(pool * 64, 64), 64)
    quarters = [pl.ds(pl.multiple_of(pool * 64 + i, 32), 32) for i in (0, 32)]
    weight_near, weight_far, twin = [], [], []

    def send_weight(p):
        c, a, b = ROT[p]
        cols = pl.ds(START[p], WIDE[p])
        src, dst = ow_ref.at[half, cols], weight[p].at[at[c], half]
        copies = group(weight[p].at[0])
        for hop in (1, 3):
            copies.push(src, dst, moved((c, hop)))
        weight_near.append(copies)
        weight[p][at[c]] = ow_ref[:, cols]

    def pass_weight(p):
        c, a, b = ROT[p]
        weight_near[p].arrived()
        copies = group(weight[p].at[0, 0:64])
        for hop, rows in ((1, quarters[0]), (3, quarters[1])):
            held = weight[p].at[plus(c, 4 - hop), rows]
            copies.push(held, held, moved((c, hop)))
        weight_far.append(copies)
        copies = group(weight[p].at[0:3, 0:64])
        for hop in (1, 3):
            held = weight[p].at[plus(c, hop), half]
            copies.push(held, held, moved(other=1))
        twin.append(copies)

    def hand_over(p):
        c, a, b = ROT[p]
        weight_far[p].arrived()
        held = weight[p].at[plus(c, 2), half]
        twin[p].push(held, held, moved(other=1))

    query_load.wait()
    key_load.wait()
    value_load.wait()
    attend()
    pl.semaphore_wait(barrier, len(partners))
    over_x, over_z = group(mid_x.at[0:3]), group(mid_z.at[0:3])
    for hop in NEAR_FIRST:
        over_x.push(att.at[plus(0, hop)], mid_x.at[at[0]], moved((0, hop)))
        over_z.push(att.at[:, plus(1, hop)], mid_z.at[at[1]], moved((1, hop)))
    ow_load.wait()
    for p in range(PARTS):
        send_weight(p)
    mid_x[at[0]] = att[at[0]]
    mid_z[at[1]] = att[:, at[1]]

    ids = iota((TOK, EXPERTS), 1)
    eye = one_hot(iota((TOK, TOK), 0) == iota((TOK, TOK), 1))
    routes = dot_nt(eye, routes_ref[...].astype(F32).astype(BF16)).astype(jnp.int32)
    chosen = routes[:, 0:1] == ids
    for k in range(1, routes.shape[1]):
        chosen = chosen | (routes[:, k : k + 1] == ids)

    def push_a(r, held):
        c, a, b = ROT[r]
        mine = held.at[at[b], at[a]]
        copies = group(held.at[0, 0:3])
        for hop in NEAR_FIRST:
            copies.push(mine, mine, moved((a, hop)))
        return copies

    def push_b(r, held):
        c, a, b = ROT[r]
        mine = held.at[at[b]]
        copies = group(held.at[0:3])
        for hop in NEAR_FIRST:
            copies.push(mine, mine, moved((b, hop)))
        return copies

    users_a, users_b = [], []
    for r in range(3):
        plane_u[r][at[ROT[r][2]], at[ROT[r][1]]] = one_hot(chosen)
        users_a.append(push_a(r, plane_u[r]))
    att_out = [group(att_in[r].at[0:3]) for r in range(3)]
    over_x.arrived()
    for hop in NEAR_FIRST:
        att_out[2].push(mid_x.at[:, plus(1, hop)], att_in[2].at[at[1]], moved((1, hop)))
        att_out[1].push(mid_x.at[:, :, plus(2, hop)], att_in[1].at[:, at[2]], moved((2, hop)))
    over_z.arrived()
    for hop in NEAR_FIRST:
        att_out[0].push(mid_z.at[:, :, plus(2, hop)], att_in[0].at[at[2]], moved((2, hop)))
    att_in[2][at[1]] = mid_x[:, at[1]]
    att_in[1][:, at[2]] = mid_x[:, :, at[2]]
    att_in[0][at[2]] = mid_z[:, :, at[2]]
    for p in range(PARTS):
        pass_weight(p)
    for r in range(3):
        users_a[r].arrived()
        users_b.append(push_b(r, plane_u[r]))
    for p in range(PARTS):
        hand_over(p)
    router_load = load(router_hbm, router_ref)
    expert_loads = [
        load(gate_hbm.at[0], gate_ref),
        load(up_hbm.at[0], up_ref),
        load(down_hbm.at[0], down_ref),
    ]

    def scatter_b(p, part, over_b):
        c, a, b = ROT[p]
        copies = group(over_b[p])
        for hop in NEAR_FIRST:
            copies.push(part[p].at[plus(b, hop)], over_b[p].at[hop - 1], moved((b, hop)))
        return copies

    def scatter_a(p, before, part, over_b, summed, over_a):
        c, a, b = ROT[p]
        before.arrived()
        total = part[p][at[b]].astype(F32)
        for i in range(3):
            total = total + over_b[p][i].astype(F32)
        summed[p][...] = total.astype(BF16)
        copies = group(over_a[p])
        for hop in NEAR_FIRST:
            copies.push(summed[p].at[plus(a, hop)], over_a[p].at[hop - 1], moved((a, hop)))
        return copies

    def scattered(p, copies, summed, over_a):
        c, a, b = ROT[p]
        copies.arrived()
        total = summed[p][at[a]].astype(F32)
        for i in range(3):
            total = total + over_a[p][i].astype(F32)
        return total

    b_out1 = []
    lhs = []
    for p in range(PARTS):
        if p < 3:
            att_out[p].arrived()
            held = att_in[p][...]
            lhs.append(
                jnp.concatenate([held[:, :, i].reshape(ALL, HD) for i in range(4)], axis=1)
            )
        twin[p].arrived()
        rhs = weight[p][...].reshape(4 * HD, WIDE[p])
        part1[p][...] = dot(lhs[p % 3], rhs).astype(BF16).reshape(4, 4, TOK, WIDE[p])
        b_out1.append(scatter_b(p, part1, over_b1))
    drain(over_x, over_z, *weight_near, *weight_far, *twin)

    same = row // TOK == col // TOK
    names, select, users = [], [], []
    for r in range(3):
        c, a, b = ROT[r]
        users_b[r].arrived()
        own = at[a] * STRIDE[a] + at[b] * STRIDE[b]
        slot = iota((ALL, EXPERTS), 0)
        expert = slot // 64 * STRIDE[c] + slot // 32 % 2 * 64 + own
        names.append(one_hot(expert == iota((ALL, EXPERTS), 1)))
        held = plane_u[r][...].reshape(ALL, EXPERTS)
        uses = dot_nt(names[r], held)
        rank = dot(uses.astype(BF16), one_hot(same & (row < col)))
        uses = (uses > 0) & (rank == (row % 2).astype(F32)) & (row // 2 % 16 == col // TOK)
        select.append(one_hot(uses))
        uses = dot_nt(held, names[r])
        rank = dot(one_hot(same & (col < row)), uses.astype(BF16))
        uses = (uses > 0) & (rank == (col % 2).astype(F32)) & (col // 2 % 16 == row // TOK)
        users.append(one_hot(uses))

    def exchange(p):
        c, a, b = ROT[p]
        b_out1[p].arrived()
        total = part1[p][at[b]].astype(F32)
        for i in range(3):
            total = total + over_b1[p][i].astype(F32)
        swap_a[p][at[a]] = total.astype(BF16)
        own = part1[p][at[b], at[a]].astype(F32)
        for i in range(3):
            own = own + over_b1[p][i, at[a]].astype(F32)
        own = own + hidden_ref[:, pl.ds(START[p], WIDE[p])].astype(F32)
        swap_a[p][at[a], at[a]] = own.astype(BF16)
        copies = group(swap_a[p].at[0:3])
        for hop in NEAR_FIRST:
            copies.push(swap_a[p].at[at[a]], swap_a[p].at[at[a]], moved((a, hop)))
        return copies

    squares, rows_b = [], []

    def finish(p):
        c, a, b = ROT[p]
        a_out1[p].arrived()
        total = swap_a[p][0].astype(F32)
        for i in range(1, 4):
            total = total + swap_a[p][i].astype(F32)
        total = total.astype(BF16).astype(F32)
        for i in range(0, WIDE[p], 128):
            j = (START[p] + i) // 128
            held = total[:, :, i : i + 128] * gain_ref[j : j + 1, :].astype(F32)
            plane[p][at[b], :, :, i : i + 128] = held.astype(BF16)
        rows_b.append(push_b(p, plane[p]))
        own = swap_a[p][0, at[a]].astype(F32)
        for i in range(1, 4):
            own = own + swap_a[p][i, at[a]].astype(F32)
        own = own.astype(BF16)
        resid[:, pl.ds(START[p], WIDE[p])] = own
        own = own.astype(F32)
        squares.append(jnp.sum(own * own, axis=-1, keepdims=True))

    hidden_load.wait()
    a_out1 = [exchange(p) for p in range(PARTS)]
    for p in range(PARTS):
        finish(p)

    scale = lax.rsqrt(sum(squares) * (1.0 / D) + 1e-06)
    for i in range(0, D, 128):
        held = resid[:, i : i + 128].astype(F32) * scale
        held = held * gain_ref[i // 128 : i // 128 + 1, :].astype(F32)
        normed[:, i : i + 128] = held.astype(BF16)
    router_load.wait()
    logits = dot(normed[...], router_ref[...])
    top = jnp.max(jnp.where(chosen, logits, -jnp.inf), axis=-1, keepdims=True)
    raised = jnp.where(chosen, jnp.exp(jnp.where(chosen, logits, top) - top), 0.0)
    shares = (raised / jnp.sum(raised, axis=-1, keepdims=True)).astype(BF16)
    lane = iota((TOK, EXPERTS), 1)
    high = scale.astype(BF16).astype(F32)
    middle = (scale - high).astype(BF16).astype(F32)
    low = scale - high - middle
    scales = jnp.where(lane == 0, high, jnp.where(lane == 1, middle, jnp.where(lane == 2, low, 0.0)))
    shares_a, shares_b = [], []
    for r in range(3):
        c, a, b = ROT[r]
        plane_w[r][at[b], at[a], :, 0:EXPERTS] = shares
        plane_w[r][at[b], at[a], :, EXPERTS : 2 * EXPERTS] = scales.astype(BF16)
        shares_a.append(push_a(r, plane_w[r]))

    def along_line(r, src, dst):
        c, a, b = ROT[r]
        copies = group(src.at[0:7])
        for step in (1, 3, 5, 7, 2, 6, 4):
            step_p, step_c = step // 4, step % 4
            there = plus(c, step_c) * 2 + lax.rem(pool + step_p, 2)
            copies.push(
                src.at[there], dst.at[at[c] * 2 + pool], moved((c, step_c), other=step_p)
            )
        dst[at[c] * 2 + pool] = src[at[c] * 2 + pool]
        return copies

    line_out = []

    def pick(p):
        rows_b[p].arrived()
        outgoing = dot(select[p % 3], plane[p][...].reshape(ALL, WIDE[p])).astype(BF16)
        picked[p][...] = outgoing.reshape(8, 32, WIDE[p])
        line_out.append(along_line(p, picked[p], rows[p]))

    for p in range(3):
        pick(p)
    for r in range(3):
        shares_a[r].arrived()
        shares_b.append(push_b(r, plane_w[r]))
    for p in range(3, PARTS):
        pick(p)
    shares_b[0].arrived()
    held = plane_w[0][...].reshape(ALL, 2 * EXPERTS)[:, EXPERTS:]
    scale_out[...] = dot(select[0], held).astype(BF16).reshape(8, 32, EXPERTS)
    scale_line = along_line(0, scale_out, scale_in)
    combine = []
    for r in range(3):
        if r:
            shares_b[r].arrived()
        held = plane_w[r][...].reshape(ALL, 2 * EXPERTS)[:, :EXPERTS]
        share = dot_nt(held, names[r])
        combine.append(jnp.where(users[r] > 0, share, 0.0).astype(BF16))
    drain(*att_out, *users_a, *users_b, *b_out1, *a_out1)
    drain(*rows_b, *shares_a, *shares_b)

    for copy in expert_loads:
        copy.wait()

    def place(slot, r):
        rank = slot % 2
        coord = {0: slot // 64, 2: slot // 8 % 4, 1: slot // 2 % 4}
        core = slot // 32 % 2
        c, a, b = ROT[r]
        return coord[c] * 64 + core * 32 + coord[b] * 8 + coord[a] * 2 + rank

    for p in range(PARTS):
        line_out[p].arrived()
        held = rows[p][...].reshape(ALL, WIDE[p])
        if p % 3:
            held = dot(one_hot(place(row, p % 3) == col), held).astype(BF16)
        cols = pl.ds(START[p], WIDE[p])
        gate = dot(held, gate_ref[cols, :])
        up = dot(held, up_ref[cols, :])
        if p:
            gate, up = gate_acc[...] + gate, up_acc[...] + up
        gate_acc[...] = gate
        up_acc[...] = up
    scale_line.arrived()
    scale = jnp.sum(scale_in[...].reshape(ALL, EXPERTS).astype(F32), axis=-1, keepdims=True)
    gate = gate_acc[...] * scale
    activated = (gate / (1.0 + jnp.exp(-gate)) * (up_acc[...] * scale)).astype(BF16)
    activated = [activated] + [
        dot(one_hot(place(col, r) == row), activated).astype(BF16) for r in (1, 2)
    ]
    line_back = []
    for p in range(PARTS):
        result = dot(activated[p % 3], down_ref[:, pl.ds(START[p], WIDE[p])]).astype(BF16)
        made[p][...] = result.reshape(8, 32, WIDE[p])
        line_back.append(along_line(p, made[p], back[p]))
    drain(scale_line, *line_out)

    b_out2 = []
    for p in range(PARTS):
        line_back[p].arrived()
        total = dot(combine[p % 3], back[p][...].reshape(ALL, WIDE[p]))
        part2[p][...] = total.astype(BF16).reshape(4, 4, TOK, WIDE[p])
        b_out2.append(scatter_b(p, part2, over_b2))
    drain(*line_back)
    a_out2 = [scatter_a(p, b_out2[p], part2, over_b2, sum2, over_a2) for p in range(PARTS)]
    drain(*b_out2)
    for p in range(PARTS):
        cols = pl.ds(START[p], WIDE[p])
        mixture = scattered(p, a_out2[p], sum2, over_a2)
        out_ref[:, cols] = (resid[:, cols].astype(F32) + mixture).astype(BF16)
    drain(*a_out2)


def shards(hidden, queries, k_cache, v_cache, o_weight, norm_gain, router_weight, w_gate, w_up, w_down, routes):
    vmem, hbm = pl.BlockSpec(memory_space=pltpu.VMEM), pl.BlockSpec(memory_space=pl.ANY)

    def parts(*lead):
        return [pltpu.VMEM((*lead, wide), BF16) for wide in WIDE]

    scratch = [
        pltpu.VMEM((TOK, D), BF16),
        pltpu.VMEM((TOK, 2 * D), BF16),
        pltpu.VMEM((D, EXPERTS), BF16),
        pltpu.VMEM((TOK, CTX, KVH * HD), BF16),
        pltpu.VMEM((TOK, CTX, KVH * HD), BF16),
        pltpu.VMEM((D, HID), BF16),
        pltpu.VMEM((D, HID), BF16),
        pltpu.VMEM((HID, D), BF16),
        pltpu.VMEM((HD, D), BF16),
        *[pltpu.VMEM((4, 4, 4, TOK, HD), BF16)] * 3,
        pltpu.VMEM((TOK, D), BF16),
        pltpu.VMEM((TOK, D), BF16),
        pltpu.VMEM((ALL, HID), F32),
        pltpu.VMEM((ALL, HID), F32),
        *[pltpu.VMEM((4, 4, 4, TOK, HD), BF16)] * 3,
        *[pltpu.VMEM((4, 4, TOK, EXPERTS), BF16)] * 3,
        *[pltpu.VMEM((4, 4, TOK, 2 * EXPERTS), BF16)] * 3,
        *[pltpu.VMEM((8, 32, EXPERTS), BF16)] * 2,
        *parts(4, HD),
        *parts(4, 4, TOK),
        *parts(3, 4, TOK),
        *parts(4, 4, TOK),
        *parts(4, 4, TOK),
        *parts(8, 32),
        *parts(8, 32),
        *parts(8, 32),
        *parts(8, 32),
        *parts(4, 4, TOK),
        *parts(3, 4, TOK),
        *parts(4, TOK),
        *parts(3, TOK),
        pltpu.SemaphoreType.DMA((N_GROUPS,)),
        pltpu.SemaphoreType.DMA((N_GROUPS,)),
        pltpu.SemaphoreType.DMA((N_LOADS,)),
    ]
    return pl.pallas_call(
        kernel,
        out_shape=jax.ShapeDtypeStruct((TOK, D), BF16),
        in_specs=[vmem] * 2 + [hbm] * 9,
        out_specs=vmem,
        scratch_shapes=scratch,
        compiler_params=pltpu.CompilerParams(
            collective_id=0, has_side_effects=True, vmem_limit_bytes=60 * 1024 * 1024
        ),
    )(
        norm_gain.reshape(D // 128, 128),
        routes.T,
        hidden,
        queries,
        router_weight,
        k_cache,
        v_cache,
        o_weight,
        w_gate,
        w_up,
        w_down,
    )


def solution(mesh):
    rows = P(("pool", "dev"), None)
    cube = P(("pool", "dev"), None, None)
    placed = (rows, rows, cube, cube, P("dev", None), P(), P(), cube, cube, cube, rows)
    return jax.shard_map(shards, mesh=mesh, in_specs=placed, out_specs=rows, check_vma=False)
```

```python
import functools
import math

import jax
import jax.numpy as jnp
from jax import lax
from jax.experimental import pallas as pl
from jax.experimental.pallas import tpu as pltpu
from jax.sharding import PartitionSpec as P

MESH = pl.DeviceIdType.MESH
F32 = jnp.float32
BF16 = jnp.bfloat16

TOK = 16
D = 4096
HD = 128
KVH = 4
CTX = 128
HID = 768
EXPERTS = 128
STRIDE = (16, 4, 1)
START = (0, 512, 1024, 1536, 2048, 2560, 2944, 3328, 3712)
WIDE = (512, 512, 512, 512, 512, 384, 384, 384, 384)
PARTS = len(WIDE)
ROT = tuple((p % 3, (p + 1) % 3, (p + 2) % 3) for p in range(PARTS))
NEAR_FIRST = (1, 3, 2)
ALL = 256


def iota(shape, dim):
    return lax.broadcasted_iota(jnp.int32, shape, dim)


def one_hot(mask):
    return jnp.where(mask, 1.0, 0.0).astype(BF16)


def dot(a, b):
    return jnp.dot(a, b, preferred_element_type=F32)


def dot_nt(a, b):
    return lax.dot_general(a, b, (((1,), (1,)), ((), ())), preferred_element_type=F32)


class Group:
    def __init__(self, sems, like):
        self.send, self.recv = sems
        self.like = like

    def push(self, src, dst, device):
        pltpu.make_async_remote_copy(
            src_ref=src,
            dst_ref=dst,
            send_sem=self.send,
            recv_sem=self.recv,
            device_id=device,
            device_id_type=MESH,
        ).start()

    def arrived(self):
        pltpu.make_async_copy(self.like, self.like, self.recv).wait()

    def sent(self):
        pltpu.make_async_copy(self.like, self.like, self.send).wait()


N_GROUPS = 10 * PARTS + 20
N_LOADS = 9


def kernel(
    gain_ref,
    routes_ref,
    hidden_hbm,
    query_hbm,
    router_hbm,
    key_hbm,
    value_hbm,
    ow_hbm,
    gate_hbm,
    up_hbm,
    down_hbm,
    out_ref,
    hidden_ref,
    query_ref,
    router_ref,
    key_ref,
    value_ref,
    gate_ref,
    up_ref,
    down_ref,
    ow_ref,
    att,
    mid_x,
    mid_z,
    resid,
    normed,
    gate_acc,
    up_acc,
    *rest,
):
    rest = list(rest)

    def take(count):
        taken = rest[:count]
        del rest[:count]
        return taken

    att_in, plane_u, plane_w = take(3), take(3), take(3)
    plane_s, scale_out, scale_in = take(3)
    weight, part1, over_b1, swap_a = [take(PARTS) for _ in range(4)]
    plane, picked, rows, made, back = [take(PARTS) for _ in range(5)]
    part2, over_b2, sum2, over_a2 = [take(PARTS) for _ in range(4)]
    send, recv, local = rest
    groups = []

    def group(like):
        i = len(groups)
        groups.append(Group((send.at[i], recv.at[i]), like))
        return groups[i]


    pool = lax.axis_index("pool")
    dev = lax.axis_index("dev")
    at = (dev // 16, (dev // 4) % 4, dev % 4)

    def moved(*steps, other=0):
        where = list(at)
        for axis, step in steps:
            where[axis] = lax.rem(at[axis] + step, 4)
        there = where[0] * 16 + where[1] * 4 + where[2]
        return (lax.rem(pool + other, 2), there)

    def plus(axis, step):
        return lax.rem(at[axis] + step, 4)

    def drain(*copies):
        for copy in copies:
            copy.sent()

    loads = []

    def load(src, dst):
        copy = pltpu.make_async_copy(src, dst, local.at[len(loads)])
        copy.start()
        loads.append(copy)
        return copy

    query_load, key_load, value_load, ow_load, hidden_load = [
        load(src, dst)
        for src, dst in (
            (query_hbm, query_ref),
            (key_hbm, key_ref),
            (value_hbm, value_ref),
            (ow_hbm, ow_ref),
            (hidden_hbm, hidden_ref),
        )
    ]

    barrier = pltpu.get_barrier_semaphore()
    partners = [moved(other=1)]
    for axis in range(3):
        for step in range(1, 4):
            partners += [moved((axis, step)), moved((axis, step), other=1)]
    for partner in partners:
        pl.semaphore_signal(barrier, inc=1, device_id=partner, device_id_type=MESH)

    row, col = iota((ALL, ALL), 0), iota((ALL, ALL), 1)
    swap = one_hot((row % TOK == col // TOK) & (row // TOK == col % TOK))

    def attend():
        empty = jnp.zeros((TOK, HD), BF16)
        asked = []
        for g in range(KVH):
            by_head = jnp.concatenate(
                [query_ref[:, (g * TOK + h) * HD : (g * TOK + h + 1) * HD] for h in range(TOK)],
                axis=0,
            )
            asked.append(dot(swap, by_head).astype(BF16))
        scores = []
        for t in range(TOK):
            rows = [
                jnp.concatenate(
                    [asked[g][t * TOK : (t + 1) * TOK] if g == i else empty for i in range(KVH)],
                    axis=1,
                )
                for g in range(KVH)
            ]
            scores.append(dot_nt(jnp.concatenate(rows, axis=0), key_ref[t]))
        scores = jnp.concatenate(scores, axis=0) * (1.0 / math.sqrt(HD))
        top = jnp.max(scores, axis=-1, keepdims=True)
        raised = jnp.exp(scores - top)
        probs = (raised / jnp.sum(raised, axis=-1, keepdims=True)).astype(BF16)
        wide = KVH * TOK
        found = [dot(probs[t * wide : (t + 1) * wide], value_ref[t]) for t in range(TOK)]
        for g in range(KVH):
            rows, lanes = slice(g * TOK, (g + 1) * TOK), slice(g * HD, (g + 1) * HD)
            attended = jnp.concatenate([held[rows, lanes] for held in found], axis=0)
            att[g] = dot(swap, attended.astype(BF16)).astype(BF16).reshape(4, 4, TOK, HD)

    half = pl.ds(pl.multiple_of(pool * 64, 64), 64)
    quarters = [pl.ds(pl.multiple_of(pool * 64 + i, 32), 32) for i in (0, 32)]
    weight_near, weight_far, twin = [], [], []

    def send_weight(p):
        c, a, b = ROT[p]
        cols = pl.ds(START[p], WIDE[p])
        src, dst = ow_ref.at[half, cols], weight[p].at[at[c], half]
        copies = group(weight[p].at[0])
        for hop in (1, 3):
            copies.push(src, dst, moved((c, hop)))
        weight_near.append(copies)
        weight[p][at[c]] = ow_ref[:, cols]

    def pass_weight(p):
        c, a, b = ROT[p]
        weight_near[p].arrived()
        copies = group(weight[p].at[0, 0:64])
        for hop, rows in ((1, quarters[0]), (3, quarters[1])):
            held = weight[p].at[plus(c, 4 - hop), rows]
            copies.push(held, held, moved((c, hop)))
        weight_far.append(copies)
        copies = group(weight[p].at[0:3, 0:64])
        for hop in (1, 3):
            held = weight[p].at[plus(c, hop), half]
            copies.push(held, held, moved(other=1))
        twin.append(copies)

    def hand_over(p):
        c, a, b = ROT[p]
        weight_far[p].arrived()
        held = weight[p].at[plus(c, 2), half]
        twin[p].push(held, held, moved(other=1))

    query_load.wait()
    key_load.wait()
    value_load.wait()
    attend()
    pl.semaphore_wait(barrier, len(partners))
    over_x, over_z = group(mid_x.at[0:3]), group(mid_z.at[0:3])
    for hop in NEAR_FIRST:
        over_x.push(att.at[plus(0, hop)], mid_x.at[at[0]], moved((0, hop)))
        over_z.push(att.at[:, plus(1, hop)], mid_z.at[at[1]], moved((1, hop)))
    ow_load.wait()
    for p in range(PARTS):
        send_weight(p)
    mid_x[at[0]] = att[at[0]]
    mid_z[at[1]] = att[:, at[1]]

    ids = iota((TOK, EXPERTS), 1)
    eye = one_hot(iota((TOK, TOK), 0) == iota((TOK, TOK), 1))
    routes = dot_nt(eye, routes_ref[...].astype(F32).astype(BF16)).astype(jnp.int32)
    chosen = routes[:, 0:1] == ids
    for k in range(1, routes.shape[1]):
        chosen = chosen | (routes[:, k : k + 1] == ids)

    def push_a(r, held):
        c, a, b = ROT[r]
        mine = held.at[at[b], at[a]]
        copies = group(held.at[0, 0:3])
        for hop in NEAR_FIRST:
            copies.push(mine, mine, moved((a, hop)))
        return copies

    def push_b(r, held):
        c, a, b = ROT[r]
        mine = held.at[at[b]]
        copies = group(held.at[0:3])
        for hop in NEAR_FIRST:
            copies.push(mine, mine, moved((b, hop)))
        return copies

    users_a, users_b = [], []
    for r in range(3):
        plane_u[r][at[ROT[r][2]], at[ROT[r][1]]] = one_hot(chosen)
        users_a.append(push_a(r, plane_u[r]))
    att_out = [group(att_in[r].at[0:3]) for r in range(3)]
    over_x.arrived()
    for hop in NEAR_FIRST:
        att_out[2].push(mid_x.at[:, plus(1, hop)], att_in[2].at[at[1]], moved((1, hop)))
        att_out[1].push(mid_x.at[:, :, plus(2, hop)], att_in[1].at[:, at[2]], moved((2, hop)))
    over_z.arrived()
    for hop in NEAR_FIRST:
        att_out[0].push(mid_z.at[:, :, plus(2, hop)], att_in[0].at[at[2]], moved((2, hop)))
    att_in[2][at[1]] = mid_x[:, at[1]]
    att_in[1][:, at[2]] = mid_x[:, :, at[2]]
    att_in[0][at[2]] = mid_z[:, :, at[2]]
    for p in range(PARTS):
        pass_weight(p)
    for r in range(3):
        users_a[r].arrived()
        users_b.append(push_b(r, plane_u[r]))
    for p in range(PARTS):
        hand_over(p)
    router_load = load(router_hbm, router_ref)
    expert_loads = [
        load(gate_hbm.at[0], gate_ref),
        load(up_hbm.at[0], up_ref),
        load(down_hbm.at[0], down_ref),
    ]

    def scatter_b(p, part, over_b):
        c, a, b = ROT[p]
        copies = group(over_b[p])
        for hop in NEAR_FIRST:
            copies.push(part[p].at[plus(b, hop)], over_b[p].at[hop - 1], moved((b, hop)))
        return copies

    def scatter_a(p, before, part, over_b, summed, over_a):
        c, a, b = ROT[p]
        before.arrived()
        total = part[p][at[b]].astype(F32)
        for i in range(3):
            total = total + over_b[p][i].astype(F32)
        summed[p][...] = total.astype(BF16)
        copies = group(over_a[p])
        for hop in NEAR_FIRST:
            copies.push(summed[p].at[plus(a, hop)], over_a[p].at[hop - 1], moved((a, hop)))
        return copies

    def scattered(p, copies, summed, over_a):
        c, a, b = ROT[p]
        copies.arrived()
        total = summed[p][at[a]].astype(F32)
        for i in range(3):
            total = total + over_a[p][i].astype(F32)
        return total

    b_out1 = []
    lhs = []
    for p in range(PARTS):
        if p < 3:
            att_out[p].arrived()
            held = att_in[p][...]
            lhs.append(
                jnp.concatenate([held[:, :, i].reshape(ALL, HD) for i in range(4)], axis=1)
            )
        twin[p].arrived()
        rhs = weight[p][...].reshape(4 * HD, WIDE[p])
        part1[p][...] = dot(lhs[p % 3], rhs).astype(BF16).reshape(4, 4, TOK, WIDE[p])
        b_out1.append(scatter_b(p, part1, over_b1))
    drain(over_x, over_z, *weight_near, *weight_far, *twin)

    same = row // TOK == col // TOK
    names, select, users = [], [], []
    for r in range(3):
        c, a, b = ROT[r]
        users_b[r].arrived()
        own = at[a] * STRIDE[a] + at[b] * STRIDE[b]
        slot = iota((ALL, EXPERTS), 0)
        expert = slot // 64 * STRIDE[c] + slot // 32 % 2 * 64 + own
        names.append(one_hot(expert == iota((ALL, EXPERTS), 1)))
        held = plane_u[r][...].reshape(ALL, EXPERTS)
        uses = dot_nt(names[r], held)
        rank = dot(uses.astype(BF16), one_hot(same & (row < col)))
        uses = (uses > 0) & (rank == (row % 2).astype(F32)) & (row // 2 % 16 == col // TOK)
        select.append(one_hot(uses))
        uses = dot_nt(held, names[r])
        rank = dot(one_hot(same & (col < row)), uses.astype(BF16))
        uses = (uses > 0) & (rank == (col % 2).astype(F32)) & (col // 2 % 16 == row // TOK)
        users.append(one_hot(uses))

    def exchange(p):
        c, a, b = ROT[p]
        b_out1[p].arrived()
        total = part1[p][at[b]].astype(F32)
        for i in range(3):
            total = total + over_b1[p][i].astype(F32)
        swap_a[p][at[a]] = total.astype(BF16)
        own = part1[p][at[b], at[a]].astype(F32)
        for i in range(3):
            own = own + over_b1[p][i, at[a]].astype(F32)
        own = own + hidden_ref[:, pl.ds(START[p], WIDE[p])].astype(F32)
        swap_a[p][at[a], at[a]] = own.astype(BF16)
        copies = group(swap_a[p].at[0:3])
        for hop in NEAR_FIRST:
            copies.push(swap_a[p].at[at[a]], swap_a[p].at[at[a]], moved((a, hop)))
        return copies

    squares, rows_b = [], []

    def finish(p):
        c, a, b = ROT[p]
        a_out1[p].arrived()
        total = swap_a[p][0].astype(F32)
        for i in range(1, 4):
            total = total + swap_a[p][i].astype(F32)
        total = total.astype(BF16).astype(F32)
        for i in range(0, WIDE[p], 128):
            j = (START[p] + i) // 128
            held = total[:, :, i : i + 128] * gain_ref[j : j + 1, :].astype(F32)
            plane[p][at[b], :, :, i : i + 128] = held.astype(BF16)
        rows_b.append(push_b(p, plane[p]))
        own = swap_a[p][0, at[a]].astype(F32)
        for i in range(1, 4):
            own = own + swap_a[p][i, at[a]].astype(F32)
        own = own.astype(BF16)
        resid[:, pl.ds(START[p], WIDE[p])] = own
        own = own.astype(F32)
        squares.append(jnp.sum(own * own, axis=-1, keepdims=True))

    hidden_load.wait()
    a_out1 = [exchange(p) for p in range(PARTS)]
    for p in range(PARTS):
        finish(p)

    scale = lax.rsqrt(sum(squares) * (1.0 / D) + 1e-06)
    lane = iota((TOK, EXPERTS), 1)
    high = scale.astype(BF16).astype(F32)
    middle = (scale - high).astype(BF16).astype(F32)
    low = scale - high - middle
    scales = jnp.where(lane == 0, high, jnp.where(lane == 1, middle, jnp.where(lane == 2, low, 0.0)))
    plane_s[at[ROT[0][2]], at[ROT[0][1]]] = scales.astype(BF16)
    scale_a = push_a(0, plane_s)
    for i in range(0, D, 128):
        held = resid[:, i : i + 128].astype(F32) * scale
        held = held * gain_ref[i // 128 : i // 128 + 1, :].astype(F32)
        normed[:, i : i + 128] = held.astype(BF16)
    router_load.wait()
    logits = dot(normed[...], router_ref[...])
    top = jnp.max(jnp.where(chosen, logits, -jnp.inf), axis=-1, keepdims=True)
    raised = jnp.where(chosen, jnp.exp(jnp.where(chosen, logits, top) - top), 0.0)
    shares = (raised / jnp.sum(raised, axis=-1, keepdims=True)).astype(BF16)
    shares_a, shares_b = [], []
    for r in range(3):
        c, a, b = ROT[r]
        plane_w[r][at[b], at[a]] = shares
        shares_a.append(push_a(r, plane_w[r]))

    def along_line(r, src, dst):
        c, a, b = ROT[r]
        copies = group(src.at[0:7])
        for step in (1, 3, 5, 7, 2, 6, 4):
            step_p, step_c = step // 4, step % 4
            there = plus(c, step_c) * 2 + lax.rem(pool + step_p, 2)
            copies.push(
                src.at[there], dst.at[at[c] * 2 + pool], moved((c, step_c), other=step_p)
            )
        dst[at[c] * 2 + pool] = src[at[c] * 2 + pool]
        return copies

    line_out = []

    def pick(p):
        rows_b[p].arrived()
        outgoing = dot(select[p % 3], plane[p][...].reshape(ALL, WIDE[p])).astype(BF16)
        picked[p][...] = outgoing.reshape(8, 32, WIDE[p])
        line_out.append(along_line(p, picked[p], rows[p]))

    for p in range(3):
        pick(p)
    scale_a.arrived()
    scale_b = push_b(0, plane_s)
    for r in range(3):
        shares_a[r].arrived()
        shares_b.append(push_b(r, plane_w[r]))
    for p in range(3, PARTS):
        pick(p)
    scale_b.arrived()
    held = plane_s[...].reshape(ALL, EXPERTS)
    scale_out[...] = dot(select[0], held).astype(BF16).reshape(8, 32, EXPERTS)
    scale_line = along_line(0, scale_out, scale_in)
    combine = []
    for r in range(3):
        shares_b[r].arrived()
        held = plane_w[r][...].reshape(ALL, EXPERTS)
        share = dot_nt(held, names[r])
        combine.append(jnp.where(users[r] > 0, share, 0.0).astype(BF16))
    drain(*att_out, *users_a, *users_b, *b_out1, *a_out1)
    drain(*rows_b, scale_a, scale_b, *shares_a, *shares_b)

    for copy in expert_loads:
        copy.wait()

    def place(slot, r):
        rank = slot % 2
        coord = {0: slot // 64, 2: slot // 8 % 4, 1: slot // 2 % 4}
        core = slot // 32 % 2
        c, a, b = ROT[r]
        return coord[c] * 64 + core * 32 + coord[b] * 8 + coord[a] * 2 + rank

    for p in range(PARTS):
        line_out[p].arrived()
        held = rows[p][...].reshape(ALL, WIDE[p])
        if p % 3:
            held = dot(one_hot(place(row, p % 3) == col), held).astype(BF16)
        cols = pl.ds(START[p], WIDE[p])
        gate = dot(held, gate_ref[cols, :])
        up = dot(held, up_ref[cols, :])
        if p:
            gate, up = gate_acc[...] + gate, up_acc[...] + up
        gate_acc[...] = gate
        up_acc[...] = up
    scale_line.arrived()
    scale = jnp.sum(scale_in[...].reshape(ALL, EXPERTS).astype(F32), axis=-1, keepdims=True)
    gate = gate_acc[...] * scale
    activated = (gate / (1.0 + jnp.exp(-gate)) * (up_acc[...] * scale)).astype(BF16)
    activated = [activated] + [
        dot(one_hot(place(col, r) == row), activated).astype(BF16) for r in (1, 2)
    ]
    line_back = []
    for p in range(PARTS):
        result = dot(activated[p % 3], down_ref[:, pl.ds(START[p], WIDE[p])]).astype(BF16)
        made[p][...] = result.reshape(8, 32, WIDE[p])
        line_back.append(along_line(p, made[p], back[p]))
    drain(scale_line, *line_out)

    b_out2 = []
    for p in range(PARTS):
        line_back[p].arrived()
        total = dot(combine[p % 3], back[p][...].reshape(ALL, WIDE[p]))
        part2[p][...] = total.astype(BF16).reshape(4, 4, TOK, WIDE[p])
        b_out2.append(scatter_b(p, part2, over_b2))
    drain(*line_back)
    a_out2 = [scatter_a(p, b_out2[p], part2, over_b2, sum2, over_a2) for p in range(PARTS)]
    drain(*b_out2)
    for p in range(PARTS):
        cols = pl.ds(START[p], WIDE[p])
        mixture = scattered(p, a_out2[p], sum2, over_a2)
        out_ref[:, cols] = (resid[:, cols].astype(F32) + mixture).astype(BF16)
    drain(*a_out2)


def shards(hidden, queries, k_cache, v_cache, o_weight, norm_gain, router_weight, w_gate, w_up, w_down, routes):
    vmem, hbm = pl.BlockSpec(memory_space=pltpu.VMEM), pl.BlockSpec(memory_space=pl.ANY)

    def parts(*lead):
        return [pltpu.VMEM((*lead, wide), BF16) for wide in WIDE]

    scratch = [
        pltpu.VMEM((TOK, D), BF16),
        pltpu.VMEM((TOK, 2 * D), BF16),
        pltpu.VMEM((D, EXPERTS), BF16),
        pltpu.VMEM((TOK, CTX, KVH * HD), BF16),
        pltpu.VMEM((TOK, CTX, KVH * HD), BF16),
        pltpu.VMEM((D, HID), BF16),
        pltpu.VMEM((D, HID), BF16),
        pltpu.VMEM((HID, D), BF16),
        pltpu.VMEM((HD, D), BF16),
        *[pltpu.VMEM((4, 4, 4, TOK, HD), BF16)] * 3,
        pltpu.VMEM((TOK, D), BF16),
        pltpu.VMEM((TOK, D), BF16),
        pltpu.VMEM((ALL, HID), F32),
        pltpu.VMEM((ALL, HID), F32),
        *[pltpu.VMEM((4, 4, 4, TOK, HD), BF16)] * 3,
        *[pltpu.VMEM((4, 4, TOK, EXPERTS), BF16)] * 3,
        *[pltpu.VMEM((4, 4, TOK, EXPERTS), BF16)] * 4,
        *[pltpu.VMEM((8, 32, EXPERTS), BF16)] * 2,
        *parts(4, HD),
        *parts(4, 4, TOK),
        *parts(3, 4, TOK),
        *parts(4, 4, TOK),
        *parts(4, 4, TOK),
        *parts(8, 32),
        *parts(8, 32),
        *parts(8, 32),
        *parts(8, 32),
        *parts(4, 4, TOK),
        *parts(3, 4, TOK),
        *parts(4, TOK),
        *parts(3, TOK),
        pltpu.SemaphoreType.DMA((N_GROUPS,)),
        pltpu.SemaphoreType.DMA((N_GROUPS,)),
        pltpu.SemaphoreType.DMA((N_LOADS,)),
    ]
    return pl.pallas_call(
        kernel,
        out_shape=jax.ShapeDtypeStruct((TOK, D), BF16),
        in_specs=[vmem] * 2 + [hbm] * 9,
        out_specs=vmem,
        scratch_shapes=scratch,
        compiler_params=pltpu.CompilerParams(
            collective_id=0, has_side_effects=True, vmem_limit_bytes=60 * 1024 * 1024
        ),
    )(
        norm_gain.reshape(D // 128, 128),
        routes.T,
        hidden,
        queries,
        router_weight,
        k_cache,
        v_cache,
        o_weight,
        w_gate,
        w_up,
        w_down,
    )


def solution(mesh):
    rows = P(("pool", "dev"), None)
    cube = P(("pool", "dev"), None, None)
    placed = (rows, rows, cube, cube, P("dev", None), P(), P(), cube, cube, cube, rows)
    return jax.shard_map(shards, mesh=mesh, in_specs=placed, out_specs=rows, check_vma=False)
```
